256 devices in a mesh: tm: 8 (over y, core), space: 32 (over z, x).
Axes of the slice: x: 4, y: 4, z: 8, core: 2. Of those that a mesh axis runs over, the one named last changes fastest.
Arguments:
- footprint: bfloat16 [4096, 32, 4096], P(('tm', 'space')), may hold values from -0.375 to 0.375
- block_tile: int32 [4096, 1], P(('tm', 'space')), may hold values from 0 to 31; in each aligned block of 16 rows (0 to 15, 16 to 31, ...) at most 2 rows name the same one
- block_sub: int32 [4096], P(('tm', 'space')), may hold values from 0 to 15
- block_rows: int32 [4096], P(('tm', 'space')), may hold values from 1 to 32, 98304 in all
- obs_var: float32 [2, 131072], P(None, ('tm', 'space')), may hold values from 0.5 to 8
- prior_std: float32 [2, 256, 65536], P(None, 'tm', 'space'), may hold values from 0.2 to 1
- ar_rate: float32 [256, 65536], P('tm', 'space'), may hold values from 0.4 to 1
- iterate: float32 [2, 131072], P(None, ('tm', 'space')), may hold values from -6 to 6
- residual: float32 [2, 131072], P(None, ('tm', 'space')), may hold values from -20 to 20
- direction: float32 [2, 131072], P(None, ('tm', 'space')), may hold values from -20 to 20
Outputs:
- new_iterate: float32 [2, 131072], P(None, ('tm', 'space'))
- new_residual: float32 [2, 131072], P(None, ('tm', 'space'))
- new_direction: float32 [2, 131072], P(None, ('tm', 'space'))
The draws below stay inside these ranges and needn't reach their ends.
Inputs may be any that keep to these rules, and one draw needn't show every extreme that they name: `block_tile`: among the blocks of one device at most 2 name the same space tile, and in every draw some device has 2 that do.
All inputs are finite; a program needn't handle non-finite values. No bound on the sum of `block_rows` on one device may be relied on, other than what follows from the above.
Results may differ from the reference program's by a relative error of at most 0.0026.
Values may be sent and summed in bfloat16 or wider, within the bound.
A program may use at most 64 MiB of HBM per device.

```python
import math
import jax
import jax.numpy as jnp
import numpy as np
from jax import lax

RHS = 2
TB = 32
BC = 128
OB = 32
SUB = 16
NBLK = 16
TILES = 32
CAP = 2
FCOL = 4096
TIME_STEP_TOTAL = 256
FLUX_CELL_TOTAL = 65536
NBLK_ALL = 4096
NOBS = 131072
N_TM = 8
N_SPACE = 32
DEVICES = 256


def draw_ar_rate(key, part):
    key = jax.random.fold_in(key, 13)
    random_keys = jax.random.split(key, 6)
    share = jax.random.uniform(random_keys[0], (), jnp.float32, 0.35, 0.65)
    slow_cell = jax.random.uniform(random_keys[1], (1, FLUX_CELL_TOTAL), jnp.float32) < share
    slow_rate = jnp.exp(-jax.random.uniform(random_keys[2], (1, FLUX_CELL_TOTAL), jnp.float32, 0.3, 1.5) / TIME_STEP_TOTAL)
    fast_rate = jax.random.uniform(random_keys[3], (1, FLUX_CELL_TOTAL), jnp.float32, 0.85, 0.93)
    baseline_rate = jnp.where(slow_cell, slow_rate, fast_rate)
    spike_moment = jax.random.uniform(random_keys[4], (TIME_STEP_TOTAL, 1), jnp.float32) < 4.0 / TIME_STEP_TOTAL
    spike_threshold = jax.random.uniform(random_keys[5], (TIME_STEP_TOTAL, FLUX_CELL_TOTAL), jnp.float32, 0.5, 0.8)
    return baseline_rate * jnp.where(spike_moment, spike_threshold, 1.0)


def ramp_scale():
    return 1.0 + 2.0 * jnp.arange(NOBS, dtype=jnp.float32) / NOBS


def draw_residual(key, part):
    key = jax.random.fold_in(key, 5)
    values = jnp.clip(jax.random.normal(key, (RHS, NOBS), jnp.float32), -6.0, 6.0)
    return values * ramp_scale()[None, :]


def draw_direction(key, part):
    key = jax.random.fold_in(key, 9)
    values = jnp.clip(jax.random.normal(key, (RHS, NOBS), jnp.float32), -6.0, 6.0)
    return values * ramp_scale()[None, :]


def set_ends(array, own_key, least, high):
    spot = [jax.random.randint(jax.random.fold_in(own_key, axis), (), 0, length) for axis, length in enumerate(array.shape)]
    longest = array.shape.index(max(array.shape))
    neighbour = spot[:longest] + [(spot[longest] + 1) % array.shape[longest]] + spot[longest + 1:]
    return array.at[tuple(spot)].set(least).at[tuple(neighbour)].set(high)


def block_scale(key, extent, cuts, smallest, largest):
    factor_of, own = 1.0, jax.random.fold_in(key, 6)
    for position, blocks in cuts:
        draws = jnp.exp(jax.random.uniform(jax.random.fold_in(own, position), (blocks,), jnp.float32, smallest / len(cuts), largest / len(cuts)))
        factor_of = factor_of * jnp.repeat(draws, extent[position] // blocks).reshape([-1 if axis == position else 1 for axis in range(len(extent))])
    return factor_of


def profile(number_of, total, most, slope):
    loads = [(1 << 20) // math.isqrt(rank ** slope) + 1 for rank in range(2, number_of + 1)]
    spare, counts = total - most - (number_of - 1), [1] * (number_of - 1)
    while spare > 0:
        movable = [i for i in range(number_of - 1) if counts[i] < most]
        pool, remaining = sum([loads[i] for i in movable]), spare
        for i in movable:
            more = min(most - counts[i], max(1, remaining * loads[i] // pool), spare)
            counts[i] = counts[i] + more
            spare = spare - more
    return np.array([most] + counts)


def ragged_sizes(key, count, total, reach, lean):
    if count == 2:
        one = jax.random.randint(key, (), max(1, total - reach), min(reach, total - 1) + 1)
        return jnp.stack([one, total - one])
    sizes = jnp.asarray(profile(count, total, reach, lean), jnp.int32)
    couples = (count - 1) // 2
    source_of, sink = sizes[1:1 + 2 * couples:2], sizes[2:2 + 2 * couples:2]
    margin = jnp.minimum(source_of - 1, reach - sink)
    shifted = jax.random.randint(jax.random.fold_in(key, 1), (couples,), 0, 1 << 20) % (margin + 1)
    sizes = sizes.at[1:1 + 2 * couples:2].set(source_of - shifted).at[2:2 + 2 * couples:2].set(sink + shifted)
    return sizes[jax.random.permutation(jax.random.fold_in(key, 2), count)]


def shared_out(own_key, own, number, rows, count, top, bound, slope):
    order = jax.random.permutation(own_key, count)
    crowded, common = shares(count, rows * top, bound, slope, True), shares(count, rows * top, bound, slope, False)
    places = jnp.arange(count)

    def named(tallies, rotation):
        used = int((tallies > 0).sum())
        fixed = max(1, used // 4)
        moved = fixed + (places - fixed + rotation * (used - fixed)) % max(1, count - fixed)
        return jnp.zeros((count,), jnp.int32).at[order[jnp.where(places < fixed, places, moved)]].set(jnp.asarray(tallies, jnp.int32))

    tallies = jnp.where(number % 4 == 0, named(crowded, number // 4), named(common, number - number // 4 - 1))
    mixed = jax.random.permutation(jax.random.fold_in(own, 3), count)
    source_of, sink = mixed[0:count // 2 * 2:2], mixed[1:count // 2 * 2:2]
    margin = jnp.minimum(tallies[source_of] - 1, bound - tallies[sink]) // 2
    margin = jnp.where((source_of == order[0]) | (sink == order[0]) | (tallies[sink] == 0), 0, jnp.maximum(margin, 0))
    moved = jax.random.randint(jax.random.fold_in(own, 4), (count // 2,), 0, 1 << 20) % (margin + 1)
    tallies = tallies.at[source_of].add(-moved).at[sink].add(moved)
    members = jnp.searchsorted(jnp.cumsum(tallies), jnp.arange(rows * top), side="right").astype(jnp.int32)
    grid = members.reshape(top, rows).T
    grid = grid[jax.random.permutation(jax.random.fold_in(own, 1), rows)]
    rotation = jax.random.randint(jax.random.fold_in(own, 2), (rows, 1), 0, top)
    return jnp.take_along_axis(grid, (jnp.arange(top)[None, :] + rotation) % top, axis=1)


def shares(count, total, most, skew, full):
    portions = [(1 << 20) // math.isqrt(standing ** skew) + 1 for standing in range(1, count + 1)]
    largest = most if full else min(most, max(-(-total // count), total * portions[0] // sum(portions)))
    least = 1 if total - largest >= count - 1 else 0
    counts, surplus = [largest] + [least] * (count - 1), total - largest - least * (count - 1)
    while surplus > 0:
        candidates = [i for i in range(1, count) if counts[i] < largest] or [i for i in range(1, count) if counts[i] < most]
        mass, left = sum([portions[i] for i in candidates]), surplus
        for i in candidates:
            addition = min(most - counts[i], max(1, left * portions[i] // mass), surplus)
            counts[i] = counts[i] + addition
            surplus = surplus - addition
    return np.array(counts)


def centred(key, shape, scale, most, cuts=(), kind=jnp.bfloat16):
    result = scale * jax.random.normal(key, shape, jnp.float32)
    if cuts:
        result = result * block_scale(key, shape, cuts, -0.22, 0.18)
    return jnp.clip(result, -most, most).astype(kind)


def setup_inputs(seed: int = 0) -> dict:
    keys = jax.random.split(jax.random.key(seed), 11)
    footprint = centred(keys[0], (NBLK_ALL, OB, FCOL), (FCOL // 16) ** -0.5, 0.375, ((0, 256),))
    block_tile_keys = jax.random.split(jax.random.fold_in(keys[1], 1), NBLK_ALL // NBLK)
    block_tile_turns = jax.random.permutation(jax.random.fold_in(keys[1], 3), NBLK_ALL // NBLK)
    block_tile = jax.vmap(lambda own, number: shared_out(jax.random.fold_in(keys[1], 2), own, number, NBLK, TILES, 1, CAP, 2))(block_tile_keys, block_tile_turns).reshape((NBLK_ALL, 1))
    block_sub = set_ends(jax.random.randint(keys[2], (NBLK_ALL,), 0, SUB), jax.random.fold_in(keys[2], 1), 0, SUB - 1).astype(jnp.int32)
    block_rows = ragged_sizes(keys[3], NBLK_ALL, NBLK_ALL * OB * 3 // 4, OB, 1).astype(jnp.int32)
    obs_var = jnp.clip(jnp.exp(math.log(8.0) - 2.7725887 * jax.random.uniform(keys[4], (RHS, NOBS), jnp.float32) ** block_scale(keys[4], (RHS, NOBS), ((1, 256),), -0.2, 0.2)), 0.5, 8.0)
    prior_std = jnp.clip(jnp.exp(math.log(1.0) - 1.609438 * jax.random.uniform(keys[5], (RHS, TIME_STEP_TOTAL, FLUX_CELL_TOTAL), jnp.float32) ** block_scale(keys[5], (RHS, TIME_STEP_TOTAL, FLUX_CELL_TOTAL), ((1, 8), (2, 32)), -0.2, 0.2)), 0.2, 1.0)
    ar_rate = draw_ar_rate(jax.random.fold_in(keys[10], 71), 0)
    iterate = centred(keys[7], (RHS, NOBS), 1.0, 6.0, ((1, 256),), jnp.float32)
    residual = draw_residual(jax.random.fold_in(keys[10], 71), 0)
    direction = draw_direction(jax.random.fold_in(keys[10], 71), 0)
    return dict(footprint=footprint, block_tile=block_tile, block_sub=block_sub, block_rows=block_rows, obs_var=obs_var, prior_std=prior_std, ar_rate=ar_rate, iterate=iterate, residual=residual, direction=direction)


def back_part(pair):
    foot_part, vec_part = pair
    return jnp.einsum("bof,rbo->brf", foot_part.astype(jnp.float32), vec_part.astype(jnp.float32)).astype(jnp.bfloat16)


def fore_part(pair):
    foot_part, flux_part = pair
    return jnp.einsum("bof,brf->rbo", foot_part.astype(jnp.float32), flux_part.astype(jnp.float32))


def reference(footprint, block_tile, block_sub, block_rows, obs_var, prior_std, ar_rate, iterate, residual, direction):
    row_index = jnp.arange(OB, dtype=jnp.int32)
    row_valid = (row_index[None, :] < block_rows[:, None]).astype(jnp.float32).reshape(-1)
    begin_iter = iterate * row_valid
    begin_res = residual * row_valid
    begin_dir = direction * row_valid
    dir_half = begin_dir.astype(jnp.bfloat16)
    block_ids = jnp.arange(NBLK_ALL, dtype=jnp.int32)
    time_block = ((block_ids // NBLK) // N_SPACE).astype(jnp.int32)
    column_block = (block_tile[:, 0] * SUB + block_sub).astype(jnp.int32)
    foot_dev = footprint.reshape(DEVICES, NBLK, OB, FCOL)
    half_dev = jnp.transpose(dir_half.reshape(RHS, DEVICES, NBLK, OB), (1, 0, 2, 3))
    contrib = lax.map(back_part, (foot_dev, half_dev)).reshape(NBLK_ALL, RHS, TB, BC)
    flux_sum = jnp.zeros((RHS, N_TM, TB, N_SPACE * SUB, BC), jnp.float32)
    flux_sum = flux_sum.at[:, time_block, :, column_block, :].add(contrib.astype(jnp.float32))
    back = flux_sum.reshape(RHS, TIME_STEP_TOTAL, FLUX_CELL_TOTAL)
    scaled = prior_std * back
    scaled_time = jnp.transpose(scaled, (1, 0, 2))

    def fwd_step(carry, inputs):
        rate_row, term_row = inputs
        state = rate_row[None, :] * carry + term_row
        return state, state

    def bwd_step(carry, inputs):
        rate_row, term_row = inputs
        state = rate_row[None, :] * (term_row + carry)
        return state, state

    zero_state = jnp.zeros((RHS, FLUX_CELL_TOTAL), jnp.float32)
    _, forward = lax.scan(fwd_step, zero_state, (ar_rate, scaled_time))
    _, backward = lax.scan(bwd_step, zero_state, (ar_rate, scaled_time), reverse=True)
    ahead = jnp.concatenate([backward[1:], jnp.zeros((1, RHS, FLUX_CELL_TOTAL), jnp.float32)], axis=0)
    flux_half = (prior_std * jnp.transpose(forward + ahead, (1, 0, 2))).astype(jnp.bfloat16)
    block_flux = flux_half.reshape(RHS, N_TM, TB, N_SPACE * SUB, BC)[:, time_block, :, column_block, :]
    block_flux = block_flux.reshape(DEVICES, NBLK, RHS, FCOL)
    projected = lax.map(fore_part, (foot_dev, block_flux))
    projected = jnp.transpose(projected, (1, 0, 2, 3)).reshape(RHS, NOBS)
    image = projected * row_valid + obs_var * begin_dir
    res_norm = jnp.sum(begin_res * begin_res, axis=1)
    curvature = jnp.sum(begin_dir * image, axis=1)
    step_size = res_norm / curvature
    new_iterate = begin_iter + step_size[:, None] * begin_dir
    new_residual = begin_res - step_size[:, None] * image
    next_norm = jnp.sum(new_residual * new_residual, axis=1)
    new_direction = new_residual + (next_norm / res_norm)[:, None] * begin_dir
    return new_iterate, new_residual, new_direction
```

```python
import functools

import jax
import jax.numpy as jnp
from jax import lax
from jax.experimental import pallas as pl
from jax.experimental.pallas import tpu as pltpu
from jax.sharding import PartitionSpec as P

MESH = pl.DeviceIdType.MESH
F32 = jnp.float32
BF16 = jnp.bfloat16

NB, OB, TB, BC, SUB, CAP = 16, 32, 32, 128, 16, 2
ROWS, COLS = NB * OB, TB * BC
HALF = 16
CHUNKS = 4


def kernel(
    n_tm, n_sp, n_x,
    btile, bsub, brows, fp_hbm, prior_hbm, ar_hbm, obs, iterate, residual, direction,
    out_iter, out_res, out_dir,
    fp, prior, rate, cbuf, prod, dep1a, dep1b, rcv1a, rcv1b, dep2a, dep2b, rcv2a, rcv2b,
    meta_out, meta_in, meta_smem, first_of, second_of, onehot, back,
    coef, ends, ends_in_a, ends_in_b, rates_own, rates_in, local, carry, fluxa, fluxb, fbuf,
    red_own, red_tm, red_sum, red_sp,
    load_sem, send_sem, recv_sem, smem_sem,
):
    me = lax.axis_index("space")
    mt = lax.axis_index("tm")
    zpos, xpos = me // n_x, me % n_x
    n_z = n_sp // n_x

    def peer(k):
        return lax.rem(zpos + k // n_x, n_z) * n_x + lax.rem(xpos + k % n_x, n_x)

    def tpeer(k):
        return lax.rem(mt + k, n_tm)

    width = COLS // CHUNKS
    loads = []
    for c in range(CHUNKS):
        part = pl.ds(c * width, width)
        loads.append(pltpu.make_async_copy(fp_hbm.at[:, part], fp.at[:, part], load_sem.at[c]))
    load_rate = pltpu.make_async_copy(ar_hbm, rate, load_sem.at[CHUNKS])
    load_prior = pltpu.make_async_copy(prior_hbm, prior, load_sem.at[CHUNKS + 1])
    for copy in loads:
        copy.start()
    load_rate.start()
    load_prior.start()

    barrier = pltpu.get_barrier_semaphore()

    def greet_space(k, _):
        pl.semaphore_signal(barrier, inc=1, device_id={"space": peer(k)}, device_id_type=MESH)
        return 0

    def greet_tm(k, _):
        pl.semaphore_signal(barrier, inc=1, device_id={"tm": tpeer(k)}, device_id_type=MESH)
        return 0

    lax.fori_loop(1, n_sp, greet_space, 0)
    lax.fori_loop(1, n_tm, greet_tm, 0)

    lane = lax.broadcasted_iota(jnp.int32, (1, ROWS), 1)
    block_of = lane // OB
    limit = jnp.zeros((1, ROWS), jnp.int32)
    for b in range(NB):
        limit = jnp.where(block_of == b, brows[b], limit)
    valid = jnp.where(lane % OB < limit, 1.0, 0.0).astype(F32)
    begin_dir = direction[...] * valid
    begin_res = residual[...] * valid

    tiles = [btile[b, 0] for b in range(NB)]
    place = []
    for b in range(NB):
        count = jnp.int32(0)
        for e in range(b):
            count = count + jnp.where(tiles[e] == tiles[b], 1, 0)
        place.append(jnp.minimum(count, CAP - 1))

    row_j = lax.broadcasted_iota(jnp.int32, (n_sp, BC), 0)
    lane_j = lax.broadcasted_iota(jnp.int32, (n_sp, BC), 1)
    place_j = (lane_j // HALF) % CAP
    wanted = jnp.full((n_sp, BC), -1, jnp.int32)
    for b in range(NB):
        wanted = jnp.where((row_j == tiles[b]) & (place_j == place[b]), bsub[b], wanted)
    meta_out[...] = (wanted * HALF + lane_j % HALF).reshape(n_sp, 1, BC)

    rowb = lax.broadcasted_iota(jnp.int32, (NB, ROWS), 0)
    spread = jnp.concatenate(
        [jnp.where(rowb == block_of, begin_dir[r : r + 1, :], 0.0) for r in range(2)], axis=0
    ).astype(BF16)
    for c in range(CHUNKS):
        loads[c].wait()

        def product(i, _):
            col = pl.multiple_of(c * width + i * 2 * BC, 2 * BC)
            got = jnp.dot(spread, fp[:, pl.ds(col, 2 * BC)], preferred_element_type=F32)
            t = c * (width // BC) + 2 * i
            cbuf[pl.ds(t, 2 * NB, stride=TB), :] = got[:, :BC]
            cbuf[pl.ds(t + 1, 2 * NB, stride=TB), :] = got[:, BC:]
            return 0

        lax.fori_loop(0, width // (2 * BC), product, 0)

    for i in range(2 * NB):
        prod[i] = cbuf[i * TB : (i + 1) * TB, :].astype(BF16)

    pl.semaphore_wait(barrier, n_sp + n_tm - 2)

    def space_copy(src, dst, j, who, s):
        return pltpu.make_async_remote_copy(
            src_ref=src.at[j], dst_ref=dst.at[who], send_sem=send_sem.at[s], recv_sem=recv_sem.at[s],
            device_id={"space": j}, device_id_type=MESH,
        )

    def tm_copy(src, dst, k, s):
        return pltpu.make_async_remote_copy(
            src_ref=src, dst_ref=dst.at[mt], send_sem=send_sem.at[s], recv_sem=recv_sem.at[s],
            device_id={"tm": k}, device_id_type=MESH,
        )

    def all_arrived(buf, count, s):
        part = buf.at[pl.ds(0, count)]
        pltpu.make_async_copy(part, part, recv_sem.at[s]).wait()

    def all_left(buf, count, s):
        part = buf.at[pl.ds(0, count)]
        pltpu.make_async_copy(part, part, send_sem.at[s]).wait()

    def send_meta(k, _):
        space_copy(meta_out, meta_in, peer(k), me, 0).start()
        return 0

    lax.fori_loop(1, n_sp, send_meta, 0)
    meta_in[me] = meta_out[me]

    def fill_first(j):
        first, second = jnp.int32(0), jnp.int32(0)
        for b in range(NB - 1, -1, -1):
            hit = btile[b, 0] == j
            second = jnp.where(hit, first, second)
            first = jnp.where(hit, b, first)
        first_of[j] = first
        second_of[j] = second
        dep1a[j, 0] = prod[first]
        dep1a[j, 1] = prod[second]

    def fill_second(j):
        dep1b[j, 0] = prod[first_of[j] + NB]
        dep1b[j, 1] = prod[second_of[j] + NB]

    def send_first(k, _):
        j = peer(k)
        fill_first(j)
        space_copy(dep1a, rcv1a, j, me, 1).start()
        return 0

    def send_second(k, _):
        j = peer(k)
        fill_second(j)
        space_copy(dep1b, rcv1b, j, me, 2).start()
        return 0

    lax.fori_loop(1, n_sp, send_first, 0)
    fill_first(me)
    rcv1a[me] = dep1a[me]
    lax.fori_loop(1, n_sp, send_second, 0)
    fill_second(me)
    rcv1b[me] = dep1b[me]

    load_rate.wait()
    row8 = lax.broadcasted_iota(jnp.int32, (8, BC), 0)

    def last(v):
        return jnp.broadcast_to(v[7:8, :], (8, BC))

    def head(v):
        return jnp.broadcast_to(v[0:1, :], (8, BC))

    def coefficients(s, _):
        cols = pl.ds(pl.multiple_of(s * BC, BC), BC)
        fcum, bcum = [], []
        for v in range(4):
            a = rate[v * 8 : (v + 1) * 8, cols]
            rows = pl.ds(v * 8, 8)
            c1 = jnp.where(row8 >= 1, a, 0.0)
            p2 = a * jnp.where(row8 >= 1, pltpu.roll(a, 1, 0), 1.0)
            c2 = jnp.where(row8 >= 2, p2, 0.0)
            p4 = p2 * jnp.where(row8 >= 2, pltpu.roll(p2, 2, 0), 1.0)
            c4 = jnp.where(row8 >= 4, p4, 0.0)
            p8 = p4 * jnp.where(row8 >= 4, pltpu.roll(p4, 4, 0), 1.0)
            d1 = jnp.where(row8 <= 6, a, 0.0)
            q2 = a * jnp.where(row8 <= 6, pltpu.roll(a, 7, 0), 1.0)
            d2 = jnp.where(row8 <= 5, q2, 0.0)
            q4 = q2 * jnp.where(row8 <= 5, pltpu.roll(q2, 6, 0), 1.0)
            d4 = jnp.where(row8 <= 3, q4, 0.0)
            q8 = q4 * jnp.where(row8 <= 3, pltpu.roll(q4, 4, 0), 1.0)
            for i, value in enumerate((c1, c2, c4, p8, d1, d2, d4, q8)):
                coef[i, s, rows, :] = value
            fcum.append(p8)
            bcum.append(q8)
        for v in range(1, 4):
            fcum[v] = fcum[v] * last(fcum[v - 1])
        for v in range(2, -1, -1):
            bcum[v] = bcum[v] * head(bcum[v + 1])
        for v in range(4):
            coef[8, s, pl.ds(v * 8, 8), :] = fcum[v]
            above = head(bcum[v + 1]) if v < 3 else jnp.ones((8, BC), F32)
            coef[9, s, pl.ds(v * 8, 8), :] = jnp.where(row8 == 7, above, pltpu.roll(bcum[v], 7, 0))
        rates_own[pl.ds(s, 1), :] = fcum[3][7:8, :]
        return 0

    lax.fori_loop(0, SUB, coefficients, 0)

    def send_rates(k, _):
        tm_copy(rates_own, rates_in, tpeer(k), 3).start()
        return 0

    lax.fori_loop(1, n_tm, send_rates, 0)
    rates_in[mt] = rates_own[...]
    load_prior.wait()

    all_arrived(meta_in, n_sp - 1, 0)
    to_smem = pltpu.make_async_copy(meta_in, meta_smem, smem_sem.at[0])
    to_smem.start()
    quarter = lax.broadcasted_iota(jnp.int32, (1, BC), 1) // (CAP * HALF)
    target = lax.broadcasted_iota(jnp.int32, (SUB * HALF, BC), 0)
    for q in range(n_sp // 4):
        key = meta_in[4 * q]
        for g in range(1, 4):
            key = jnp.where(quarter == g, meta_in[4 * q + g], key)
        onehot[:, q * BC : (q + 1) * BC] = jnp.where(target == key, 1.0, 0.0).astype(BF16)
    to_smem.wait()
    all_arrived(rates_in, n_tm - 1, 3)

    def owner(r, rcv, flux, dep2, ends_in, s_in, s_ends, s_out):
        all_arrived(rcv, n_sp - 1, s_in)
        for h in range(2):
            part = rcv[:, :, h * HALF : (h + 1) * HALF, :].reshape(n_sp * CAP * HALF, BC)
            back[h] = jnp.dot(onehot[...], part, preferred_element_type=F32)

        def recursions(s, _):
            cols = pl.ds(pl.multiple_of(s * BC, BC), BC)
            fwd, bwd = [], []
            for v in range(4):
                rows = pl.ds(v * 8, 8)
                start = pl.multiple_of(s * HALF + (v % 2) * 8, 8)
                term = prior[r, v * 8 : (v + 1) * 8, cols] * back[v // 2, pl.ds(start, 8), :]
                y = term + coef[0, s, rows, :] * pltpu.roll(term, 1, 0)
                y = y + coef[1, s, rows, :] * pltpu.roll(y, 2, 0)
                y = y + coef[2, s, rows, :] * pltpu.roll(y, 4, 0)
                w = term * rate[v * 8 : (v + 1) * 8, cols]
                w = w + coef[4, s, rows, :] * pltpu.roll(w, 7, 0)
                w = w + coef[5, s, rows, :] * pltpu.roll(w, 6, 0)
                w = w + coef[6, s, rows, :] * pltpu.roll(w, 4, 0)
                fwd.append(y)
                bwd.append(w)
            for v in range(1, 4):
                fwd[v] = fwd[v] + coef[3, s, pl.ds(v * 8, 8), :] * last(fwd[v - 1])
            for v in range(2, -1, -1):
                bwd[v] = bwd[v] + coef[7, s, pl.ds(v * 8, 8), :] * head(bwd[v + 1])
            for v in range(4):
                above = head(bwd[v + 1]) if v < 3 else jnp.zeros((8, BC), F32)
                ahead = jnp.where(row8 == 7, above, pltpu.roll(bwd[v], 7, 0))
                local[s, pl.ds(v * 8, 8), :] = fwd[v] + ahead
            ends[r, 0, pl.ds(s, 1), :] = fwd[3][7:8, :]
            ends[r, 1, pl.ds(s, 1), :] = bwd[0][0:1, :]
            return 0

        lax.fori_loop(0, SUB, recursions, 0)

        def send_ends(k, _):
            who = tpeer(k)
            tm_copy(ends.at[r, jnp.where(who > mt, 0, 1)], ends_in, who, s_ends).start()
            return 0

        lax.fori_loop(1, n_tm, send_ends, 0)
        ends_in[mt] = jnp.zeros((SUB, BC), F32)
        all_arrived(ends_in, n_tm - 1, s_ends)
        below = jnp.zeros((SUB, BC), F32)
        for i in range(n_tm - 1):
            below = jnp.where(i < mt, rates_in[i] * below + ends_in[i], below)
        above = jnp.zeros((SUB, BC), F32)
        for i in range(n_tm - 1, 0, -1):
            above = jnp.where(i > mt, rates_in[i] * above + ends_in[i], above)
        carry[0] = below
        carry[1] = above

        def finish(s, _):
            cols = pl.ds(pl.multiple_of(s * BC, BC), BC)
            total = (
                local[s]
                + coef[8, s] * carry[0, pl.ds(s, 1), :]
                + coef[9, s] * carry[1, pl.ds(s, 1), :]
            )
            flux[s] = (prior[r, :, cols] * total).astype(BF16)
            return 0

        lax.fori_loop(0, SUB, finish, 0)

        def fill(j):
            for p in range(CAP):
                dep2[j, p] = flux[jnp.maximum(meta_smem[j, 0, p * HALF], 0) // HALF]

        def send_flux(k, _):
            j = peer(k)
            fill(j)
            space_copy(dep2, rcv2a if r == 0 else rcv2b, j, me, s_out).start()
            return 0

        lax.fori_loop(1, n_sp, send_flux, 0)
        fill(me)
        (rcv2a if r == 0 else rcv2b)[me] = dep2[me]

    owner(0, rcv1a, fluxa, dep2a, ends_in_a, 1, 4, 6)
    owner(1, rcv1b, fluxb, dep2b, ends_in_b, 2, 5, 7)

    images = []
    for r, (rcv, s_out) in enumerate(((rcv2a, 6), (rcv2b, 7))):
        all_arrived(rcv, n_sp - 1, s_out)
        for b in range(NB):
            fbuf[b * TB : (b + 1) * TB, :] = rcv[tiles[b], place[b]].astype(F32)

        def project(i, total):
            col = pl.multiple_of(i * 2 * BC, 2 * BC)
            left = jnp.concatenate(
                [fbuf[pl.ds(2 * i, NB, stride=TB), :], fbuf[pl.ds(2 * i + 1, NB, stride=TB), :]], axis=1
            ).astype(BF16)
            return total + lax.dot_general(
                left, fp[:, pl.ds(col, 2 * BC)], (((1,), (1,)), ((), ())), preferred_element_type=F32
            )

        total = lax.fori_loop(0, TB // 2, project, jnp.zeros((NB, ROWS), F32))
        images.append(jnp.sum(jnp.where(rowb == block_of, total, 0.0), axis=0, keepdims=True))
    image = jnp.concatenate(images, axis=0) * valid + obs[...] * begin_dir

    def partial(value):
        total = value[:, :BC]
        for i in range(1, ROWS // BC):
            total = total + value[:, i * BC : (i + 1) * BC]
        return total

    mine = jnp.concatenate(
        [
            partial(begin_res * begin_res),
            partial(begin_dir * image),
            partial(begin_res * image),
            partial(image * image),
        ],
        axis=0,
    )
    red_own[...] = mine
    red_tm[mt] = mine

    def send_tm_sum(k, _):
        tm_copy(red_own, red_tm, tpeer(k), 8).start()
        return 0

    lax.fori_loop(1, n_tm, send_tm_sum, 0)
    all_arrived(red_tm, n_tm - 1, 8)
    part = red_tm[0]
    for i in range(1, n_tm):
        part = part + red_tm[i]
    red_sum[...] = part
    red_sp[me] = part

    def send_sp_sum(k, _):
        j = peer(k)
        pltpu.make_async_remote_copy(
            src_ref=red_sum, dst_ref=red_sp.at[me], send_sem=send_sem.at[9], recv_sem=recv_sem.at[9],
            device_id={"space": j}, device_id_type=MESH,
        ).start()
        return 0

    lax.fori_loop(1, n_sp, send_sp_sum, 0)
    all_arrived(red_sp, n_sp - 1, 9)
    whole = jnp.sum(jnp.sum(red_sp[...], axis=0), axis=1, keepdims=True)
    res_norm, curvature, cross, square = (whole[2 * i : 2 * i + 2, :] for i in range(4))
    step = res_norm / curvature
    next_norm = res_norm - 2.0 * step * cross + step * step * square
    new_res = begin_res - step * image
    out_iter[...] = iterate[...] * valid + step * begin_dir
    out_res[...] = new_res
    out_dir[...] = new_res + (next_norm / res_norm) * begin_dir

    all_left(meta_out, n_sp - 1, 0)
    all_left(dep1a, n_sp - 1, 1)
    all_left(dep1b, n_sp - 1, 2)
    all_left(rates_in, n_tm - 1, 3)
    all_left(ends_in_a, n_tm - 1, 4)
    all_left(ends_in_b, n_tm - 1, 5)
    all_left(dep2a, n_sp - 1, 6)
    all_left(dep2b, n_sp - 1, 7)
    all_left(red_tm, n_tm - 1, 8)
    all_left(red_sp, n_sp - 1, 9)


def solution(mesh):
    n_tm, n_sp = mesh.shape["tm"], mesh.shape["space"]
    n_x = 4

    def per_device(footprint, block_tile, block_sub, block_rows, obs_var, prior_std, ar_rate, iterate, residual, direction):
        vmem = pl.BlockSpec(memory_space=pltpu.VMEM)
        smem = pl.BlockSpec(memory_space=pltpu.SMEM)
        hbm = pl.BlockSpec(memory_space=pl.ANY)
        slots = pltpu.VMEM((n_sp, CAP, TB, BC), BF16)
        state = pltpu.VMEM((n_tm, SUB, BC), F32)
        vector = jax.ShapeDtypeStruct(iterate.shape, F32)
        return pl.pallas_call(
            functools.partial(kernel, n_tm, n_sp, n_x),
            out_shape=(vector, vector, vector),
            in_specs=[smem, smem, smem, hbm, hbm, hbm, vmem, vmem, vmem, vmem],
            out_specs=(vmem, vmem, vmem),
            scratch_shapes=[
                pltpu.VMEM((ROWS, COLS), BF16),
                pltpu.VMEM(prior_std.shape, F32),
                pltpu.VMEM(ar_rate.shape, F32),
                pltpu.VMEM((2 * NB * TB, BC), F32),
                pltpu.VMEM((2 * NB, TB, BC), BF16),
                slots, slots, slots, slots, slots, slots, slots, slots,
                pltpu.VMEM((n_sp, 1, BC), jnp.int32),
                pltpu.VMEM((n_sp, 1, BC), jnp.int32),
                pltpu.SMEM((n_sp, 1, BC), jnp.int32),
                pltpu.SMEM((n_sp,), jnp.int32),
                pltpu.SMEM((n_sp,), jnp.int32),
                pltpu.VMEM((SUB * HALF, n_sp * CAP * HALF), BF16),
                pltpu.VMEM((2, SUB * HALF, BC), F32),
                pltpu.VMEM((10, SUB, TB, BC), F32),
                pltpu.VMEM((2, 2, SUB, BC), F32),
                state, state,
                pltpu.VMEM((SUB, BC), F32),
                state,
                pltpu.VMEM((SUB, TB, BC), F32),
                pltpu.VMEM((2, SUB, BC), F32),
                pltpu.VMEM((SUB, TB, BC), BF16),
                pltpu.VMEM((SUB, TB, BC), BF16),
                pltpu.VMEM((NB * TB, BC), F32),
                pltpu.VMEM((8, BC), F32),
                pltpu.VMEM((n_tm, 8, BC), F32),
                pltpu.VMEM((8, BC), F32),
                pltpu.VMEM((n_sp, 8, BC), F32),
                pltpu.SemaphoreType.DMA((CHUNKS + 2,)),
                pltpu.SemaphoreType.DMA((10,)),
                pltpu.SemaphoreType.DMA((10,)),
                pltpu.SemaphoreType.DMA((1,)),
            ],
            compiler_params=pltpu.CompilerParams(
                collective_id=0, has_side_effects=True, vmem_limit_bytes=40 << 20
            ),
            name="cg_step",
        )(
            block_tile, block_sub, block_rows, footprint.reshape(ROWS, COLS), prior_std, ar_rate,
            obs_var, iterate, residual, direction,
        )

    return jax.shard_map(
        per_device,
        mesh=mesh,
        in_specs=(
            P(("tm", "space"), None, None),
            P(("tm", "space"), None),
            P(("tm", "space")),
            P(("tm", "space")),
            P(None, ("tm", "space")),
            P(None, "tm", "space"),
            P("tm", "space"),
            P(None, ("tm", "space")),
            P(None, ("tm", "space")),
            P(None, ("tm", "space")),
        ),
        out_specs=(P(None, ("tm", "space")), P(None, ("tm", "space")), P(None, ("tm", "space"))),
        check_vma=False,
    )
```

```python
import functools

import jax
import jax.numpy as jnp
from jax import lax
from jax.experimental import pallas as pl
from jax.experimental.pallas import tpu as pltpu
from jax.sharding import PartitionSpec as P

MESH = pl.DeviceIdType.MESH
F32 = jnp.float32
BF16 = jnp.bfloat16

NB, OB, TB, BC, SUB, CAP = 16, 32, 32, 128, 16, 2
ROWS, COLS = NB * OB, TB * BC
HALF = 16
CHUNKS = 4


def kernel(
    n_tm, n_sp, n_x,
    btile_hbm, bsub_hbm, brows_hbm, fp_hbm, prior_hbm, ar_hbm, obs_hbm, iter_hbm, res_hbm, dir_hbm,
    out_iter, out_res, out_dir, out_image, out_step, out_ratio,
    btile, bsub, brows, obs, iterate, residual, direction,
    fp, wide_fp, accum, prior, rate, cbuf, prod, dep1a, dep1b, rcv1a, rcv1b, dep2a, dep2b, rcv2a, rcv2b,
    meta_out, meta_in, meta_smem, first_of, second_of, onehot, back,
    coef, ends, ends_in_a, ends_in_b, rates_own, rates_in, local, carry, fluxa, fluxb, fbuf,
    red_own, red_tm, red_sum, red_sp,
    load_sem, send_sem, recv_sem, smem_sem,
):
    me = lax.axis_index("space")
    mt = lax.axis_index("tm")
    zpos, xpos = me // n_x, me % n_x
    n_z = n_sp // n_x

    def peer(k):
        i = k // n_x
        away = n_z // 2 + (i + 1) // 2 * (1 - 2 * (i % 2))
        return lax.rem(zpos + away, n_z) * n_x + lax.rem(xpos + n_x - 1 - k % n_x, n_x)

    def tpeer(k):
        return lax.rem(mt + k, n_tm)

    width = COLS // CHUNKS
    loads = []
    for c in range(CHUNKS):
        part = pl.ds(c * width, width)
        loads.append(pltpu.make_async_copy(fp_hbm.at[:, part], fp.at[:, part], load_sem.at[c]))
    load_rate = pltpu.make_async_copy(ar_hbm, rate, load_sem.at[CHUNKS])
    load_prior = pltpu.make_async_copy(prior_hbm, prior, load_sem.at[CHUNKS + 1])
    small = [
        pltpu.make_async_copy(src, dst, load_sem.at[CHUNKS + 2 + i])
        for i, (src, dst) in enumerate(
            (
                (btile_hbm, btile), (bsub_hbm, bsub), (brows_hbm, brows), (dir_hbm, direction),
                (res_hbm, residual), (iter_hbm, iterate), (obs_hbm, obs),
            )
        )
    ]
    for copy in small[:4]:
        copy.start()
    for copy in loads:
        copy.start()
    for copy in small[4:]:
        copy.start()
    load_rate.start()
    load_prior.start()

    barrier = pltpu.get_barrier_semaphore()

    def greet_space(k, _):
        pl.semaphore_signal(barrier, inc=1, device_id={"space": peer(k)}, device_id_type=MESH)
        return 0

    def greet_tm(k, _):
        pl.semaphore_signal(barrier, inc=1, device_id={"tm": tpeer(k)}, device_id_type=MESH)
        return 0

    lax.fori_loop(0, n_sp - 1, greet_space, 0)
    lax.fori_loop(1, n_tm, greet_tm, 0)

    for copy in small:
        copy.wait()

    lane = lax.broadcasted_iota(jnp.int32, (1, ROWS), 1)
    block_of = lane // OB
    limit = jnp.zeros((1, ROWS), jnp.int32)
    for b in range(NB):
        limit = jnp.where(block_of == b, brows[b], limit)
    valid = jnp.where(lane % OB < limit, 1.0, 0.0).astype(F32)
    begin_dir = direction[...] * valid
    begin_res = residual[...] * valid

    tiles = [btile[b] for b in range(NB)]
    place = []
    for b in range(NB):
        count = jnp.int32(0)
        for e in range(b):
            count = count + jnp.where(tiles[e] == tiles[b], 1, 0)
        place.append(jnp.minimum(count, CAP - 1))

    row_j = lax.broadcasted_iota(jnp.int32, (n_sp, BC), 0)
    lane_j = lax.broadcasted_iota(jnp.int32, (n_sp, BC), 1)
    place_j = (lane_j // HALF) % CAP
    wanted = jnp.full((n_sp, BC), -1, jnp.int32)
    for b in range(NB):
        wanted = jnp.where((row_j == tiles[b]) & (place_j == place[b]), bsub[b], wanted)
    meta_out[...] = (wanted * HALF + lane_j % HALF).reshape(n_sp, 1, BC)

    def find(j, _):
        first, second = jnp.int32(0), jnp.int32(0)
        for b in range(NB - 1, -1, -1):
            hit = btile[b] == j
            second = jnp.where(hit, first, second)
            first = jnp.where(hit, b, first)
        first_of[j] = first
        second_of[j] = second
        return 0

    lax.fori_loop(0, n_sp, find, 0)

    rowb = lax.broadcasted_iota(jnp.int32, (NB, ROWS), 0)
    spread = jnp.concatenate(
        [jnp.where(rowb == block_of, begin_dir[r : r + 1, :], 0.0) for r in range(2)], axis=0
    ).astype(BF16)
    for c in range(CHUNKS):
        loads[c].wait()

        def product(i, _):
            col = pl.multiple_of(c * width + i * 2 * BC, 2 * BC)
            got = jnp.dot(spread, fp[:, pl.ds(col, 2 * BC)], preferred_element_type=F32)
            t = c * (width // BC) + 2 * i
            cbuf[pl.ds(t, 2 * NB, stride=TB), :] = got[:, :BC]
            cbuf[pl.ds(t + 1, 2 * NB, stride=TB), :] = got[:, BC:]
            return 0

        lax.fori_loop(0, width // (2 * BC), product, 0)

    for i in range(2 * NB):
        prod[i] = cbuf[i * TB : (i + 1) * TB, :].astype(BF16)

    pl.semaphore_wait(barrier, n_sp + n_tm - 2)

    def space_copy(src, dst, j, who, s):
        return pltpu.make_async_remote_copy(
            src_ref=src.at[j], dst_ref=dst.at[who], send_sem=send_sem.at[s], recv_sem=recv_sem.at[s],
            device_id={"space": j}, device_id_type=MESH,
        )

    def tm_copy(src, dst, k, s):
        return pltpu.make_async_remote_copy(
            src_ref=src, dst_ref=dst.at[mt], send_sem=send_sem.at[s], recv_sem=recv_sem.at[s],
            device_id={"tm": k}, device_id_type=MESH,
        )

    def all_arrived(buf, count, s):
        part = buf.at[pl.ds(0, count)]
        pltpu.make_async_copy(part, part, recv_sem.at[s]).wait()

    def all_left(buf, count, s):
        part = buf.at[pl.ds(0, count)]
        pltpu.make_async_copy(part, part, send_sem.at[s]).wait()

    def send_meta(k, _):
        space_copy(meta_out, meta_in, peer(k), me, 0).start()
        return 0

    lax.fori_loop(0, n_sp - 1, send_meta, 0)
    meta_in[me] = meta_out[me]

    def fill_first(j):
        dep1a[j, 0] = prod[first_of[j]]
        dep1a[j, 1] = prod[second_of[j]]

    def fill_second(j):
        dep1b[j, 0] = prod[first_of[j] + NB]
        dep1b[j, 1] = prod[second_of[j] + NB]

    def send_first(k, _):
        j = peer(k)
        fill_first(j)
        space_copy(dep1a, rcv1a, j, me, 1).start()
        return 0

    def send_second(k, _):
        j = peer(k)
        fill_second(j)
        space_copy(dep1b, rcv1b, j, me, 2).start()
        return 0

    lax.fori_loop(0, n_sp - 1, send_first, 0)
    fill_first(me)
    rcv1a[me] = dep1a[me]
    lax.fori_loop(0, n_sp - 1, send_second, 0)
    fill_second(me)
    rcv1b[me] = dep1b[me]

    load_rate.wait()
    row8 = lax.broadcasted_iota(jnp.int32, (8, BC), 0)

    def last(v):
        return jnp.broadcast_to(v[7:8, :], (8, BC))

    def head(v):
        return jnp.broadcast_to(v[0:1, :], (8, BC))

    def coefficients(s, _):
        cols = pl.ds(pl.multiple_of(s * BC, BC), BC)
        fcum, bcum = [], []
        for v in range(4):
            a = rate[v * 8 : (v + 1) * 8, cols]
            rows = pl.ds(v * 8, 8)
            c1 = jnp.where(row8 >= 1, a, 0.0)
            p2 = a * jnp.where(row8 >= 1, pltpu.roll(a, 1, 0), 1.0)
            c2 = jnp.where(row8 >= 2, p2, 0.0)
            p4 = p2 * jnp.where(row8 >= 2, pltpu.roll(p2, 2, 0), 1.0)
            c4 = jnp.where(row8 >= 4, p4, 0.0)
            p8 = p4 * jnp.where(row8 >= 4, pltpu.roll(p4, 4, 0), 1.0)
            d1 = jnp.where(row8 <= 6, a, 0.0)
            q2 = a * jnp.where(row8 <= 6, pltpu.roll(a, 7, 0), 1.0)
            d2 = jnp.where(row8 <= 5, q2, 0.0)
            q4 = q2 * jnp.where(row8 <= 5, pltpu.roll(q2, 6, 0), 1.0)
            d4 = jnp.where(row8 <= 3, q4, 0.0)
            q8 = q4 * jnp.where(row8 <= 3, pltpu.roll(q4, 4, 0), 1.0)
            for i, value in enumerate((c1, c2, c4, p8, d1, d2, d4, q8)):
                coef[i, s, rows, :] = value
            fcum.append(p8)
            bcum.append(q8)
        for v in range(1, 4):
            fcum[v] = fcum[v] * last(fcum[v - 1])
        for v in range(2, -1, -1):
            bcum[v] = bcum[v] * head(bcum[v + 1])
        for v in range(4):
            coef[8, s, pl.ds(v * 8, 8), :] = fcum[v]
            above = head(bcum[v + 1]) if v < 3 else jnp.ones((8, BC), F32)
            coef[9, s, pl.ds(v * 8, 8), :] = jnp.where(row8 == 7, above, pltpu.roll(bcum[v], 7, 0))
        rates_own[pl.ds(s, 1), :] = fcum[3][7:8, :]
        return 0

    lax.fori_loop(0, SUB, coefficients, 0)

    def send_rates(k, _):
        tm_copy(rates_own, rates_in, tpeer(k), 3).start()
        return 0

    lax.fori_loop(1, n_tm, send_rates, 0)
    rates_in[mt] = rates_own[...]
    load_prior.wait()

    def widen(t, _):
        at = pl.ds(pl.multiple_of(t * BC, BC), BC)
        wide_fp[:, at] = fp[:, at].astype(F32)
        return 0

    lax.fori_loop(0, TB, widen, 0)

    all_arrived(meta_in, n_sp - 1, 0)
    to_smem = pltpu.make_async_copy(meta_in, meta_smem, smem_sem.at[0])
    to_smem.start()
    quarter = lax.broadcasted_iota(jnp.int32, (1, BC), 1) // (CAP * HALF)
    target = lax.broadcasted_iota(jnp.int32, (SUB * HALF, BC), 0)
    for q in range(n_sp // 4):
        key = meta_in[4 * q]
        for g in range(1, 4):
            key = jnp.where(quarter == g, meta_in[4 * q + g], key)
        onehot[:, q * BC : (q + 1) * BC] = jnp.where(target == key, 1.0, 0.0).astype(BF16)
    to_smem.wait()
    all_arrived(rates_in, n_tm - 1, 3)

    def owner(r, rcv, flux, dep2, ends_in, s_in, s_ends, s_out):
        all_arrived(rcv, n_sp - 1, s_in)
        for h in range(2):
            part = rcv[:, :, h * HALF : (h + 1) * HALF, :].reshape(n_sp * CAP * HALF, BC)
            back[h] = jnp.dot(onehot[...], part, preferred_element_type=F32)

        def recursions(s, _):
            cols = pl.ds(pl.multiple_of(s * BC, BC), BC)
            fwd, bwd = [], []
            for v in range(4):
                rows = pl.ds(v * 8, 8)
                start = pl.multiple_of(s * HALF + (v % 2) * 8, 8)
                term = prior[r, v * 8 : (v + 1) * 8, cols] * back[v // 2, pl.ds(start, 8), :]
                y = term + coef[0, s, rows, :] * pltpu.roll(term, 1, 0)
                y = y + coef[1, s, rows, :] * pltpu.roll(y, 2, 0)
                y = y + coef[2, s, rows, :] * pltpu.roll(y, 4, 0)
                w = term * rate[v * 8 : (v + 1) * 8, cols]
                w = w + coef[4, s, rows, :] * pltpu.roll(w, 7, 0)
                w = w + coef[5, s, rows, :] * pltpu.roll(w, 6, 0)
                w = w + coef[6, s, rows, :] * pltpu.roll(w, 4, 0)
                fwd.append(y)
                bwd.append(w)
            for v in range(1, 4):
                fwd[v] = fwd[v] + coef[3, s, pl.ds(v * 8, 8), :] * last(fwd[v - 1])
            for v in range(2, -1, -1):
                bwd[v] = bwd[v] + coef[7, s, pl.ds(v * 8, 8), :] * head(bwd[v + 1])
            for v in range(4):
                above = head(bwd[v + 1]) if v < 3 else jnp.zeros((8, BC), F32)
                ahead = jnp.where(row8 == 7, above, pltpu.roll(bwd[v], 7, 0))
                local[s, pl.ds(v * 8, 8), :] = fwd[v] + ahead
            ends[r, 0, pl.ds(s, 1), :] = fwd[3][7:8, :]
            ends[r, 1, pl.ds(s, 1), :] = bwd[0][0:1, :]
            return 0

        lax.fori_loop(0, SUB, recursions, 0, unroll=2)

        def send_ends(k, _):
            who = tpeer(k)
            tm_copy(ends.at[r, jnp.where(who > mt, 0, 1)], ends_in, who, s_ends).start()
            return 0

        lax.fori_loop(1, n_tm, send_ends, 0)
        ends_in[mt] = jnp.zeros((SUB, BC), F32)
        all_arrived(ends_in, n_tm - 1, s_ends)
        below = jnp.zeros((SUB, BC), F32)
        for i in range(n_tm - 1):
            below = jnp.where(i < mt, rates_in[i] * below + ends_in[i], below)
        above = jnp.zeros((SUB, BC), F32)
        for i in range(n_tm - 1, 0, -1):
            above = jnp.where(i > mt, rates_in[i] * above + ends_in[i], above)
        carry[0] = below
        carry[1] = above

        def finish(s, _):
            cols = pl.ds(pl.multiple_of(s * BC, BC), BC)
            total = (
                local[s]
                + coef[8, s] * carry[0, pl.ds(s, 1), :]
                + coef[9, s] * carry[1, pl.ds(s, 1), :]
            )
            flux[s] = (prior[r, :, cols] * total).astype(BF16)
            return 0

        lax.fori_loop(0, SUB, finish, 0, unroll=2)

        def fill(j):
            for p in range(CAP):
                dep2[j, p] = flux[jnp.maximum(meta_smem[j, 0, p * HALF], 0) // HALF]

        def send_flux(k, _):
            j = peer(k)
            fill(j)
            space_copy(dep2, rcv2a if r == 0 else rcv2b, j, me, s_out).start()
            return 0

        lax.fori_loop(0, n_sp - 1, send_flux, 0)
        fill(me)
        (rcv2a if r == 0 else rcv2b)[me] = dep2[me]

    owner(0, rcv1a, fluxa, dep2a, ends_in_a, 1, 4, 6)
    owner(1, rcv1b, fluxb, dep2b, ends_in_b, 2, 5, 7)

    images = []
    for r, (rcv, s_out) in enumerate(((rcv2a, 6), (rcv2b, 7))):
        all_arrived(rcv, n_sp - 1, s_out)
        for b in range(NB):
            fbuf[b * TB : (b + 1) * TB, :] = rcv[tiles[b], place[b]].astype(F32)

        def project(b, _):
            own = pl.ds(pl.multiple_of(b * OB, OB), OB)
            total = jnp.zeros((OB, BC), F32)
            for t in range(TB):
                total = total + wide_fp[own, t * BC : (t + 1) * BC] * fbuf[pl.ds(b * TB + t, 1), :]
            accum[own, :] = total
            return 0

        lax.fori_loop(0, NB, project, 0, unroll=2)
        images.append(
            jnp.concatenate(
                [
                    jnp.sum(accum[i * BC : (i + 1) * BC, :].T, axis=0, keepdims=True)
                    for i in range(ROWS // BC)
                ],
                axis=1,
            )
        )
    image = jnp.concatenate(images, axis=0) * valid + obs[...] * begin_dir

    def partial(value):
        total = value[:, :BC]
        for i in range(1, ROWS // BC):
            total = total + value[:, i * BC : (i + 1) * BC]
        return total

    mine = jnp.concatenate(
        [
            partial(begin_res * begin_res),
            partial(begin_dir * image),
            partial(begin_res * image),
            partial(image * image),
        ],
        axis=0,
    )
    lane8 = lax.broadcasted_iota(jnp.int32, (8, BC), 1)
    row8 = lax.broadcasted_iota(jnp.int32, (8, BC), 0)

    def as_row(column):
        return jnp.sum(jnp.where(lane8 == row8, column, 0.0), axis=0, keepdims=True)

    mine = as_row(jnp.sum(mine, axis=1, keepdims=True))
    red_own[...] = mine
    red_tm[mt] = mine

    def send_tm_sum(k, _):
        tm_copy(red_own, red_tm, tpeer(k), 8).start()
        return 0

    lax.fori_loop(1, n_tm, send_tm_sum, 0)
    all_arrived(red_tm, n_tm - 1, 8)
    part = red_tm[0]
    for i in range(1, n_tm):
        part = part + red_tm[i]
    red_sum[...] = part
    red_sp[me] = part

    def send_sp_sum(k, _):
        pltpu.make_async_remote_copy(
            src_ref=red_sum, dst_ref=red_sp.at[me], send_sem=send_sem.at[9], recv_sem=recv_sem.at[9],
            device_id={"space": peer(k)}, device_id_type=MESH,
        ).start()
        return 0

    lax.fori_loop(0, n_sp - 1, send_sp_sum, 0)
    all_arrived(red_sp, n_sp - 1, 9)
    whole = jnp.broadcast_to(jnp.sum(red_sp[...], axis=0), (8, BC))
    whole = jnp.sum(jnp.where(lane8 == row8, whole, 0.0), axis=1, keepdims=True)
    res_norm, curvature, cross, square = (whole[2 * i : 2 * i + 2, :] for i in range(4))
    step = res_norm / curvature
    next_norm = res_norm - 2.0 * step * cross + step * step * square
    wide = begin_dir.shape
    out_iter[...] = iterate[...] * valid
    out_res[...] = begin_res
    out_dir[...] = begin_dir
    out_image[...] = image
    out_step[...] = jnp.broadcast_to(step, wide)
    out_ratio[...] = jnp.broadcast_to(next_norm / res_norm, wide)

    all_left(meta_out, n_sp - 1, 0)
    all_left(dep1a, n_sp - 1, 1)
    all_left(dep1b, n_sp - 1, 2)
    all_left(rates_in, n_tm - 1, 3)
    all_left(ends_in_a, n_tm - 1, 4)
    all_left(ends_in_b, n_tm - 1, 5)
    all_left(dep2a, n_sp - 1, 6)
    all_left(dep2b, n_sp - 1, 7)
    all_left(red_tm, n_tm - 1, 8)
    all_left(red_sp, n_sp - 1, 9)


def solution(mesh):
    n_tm, n_sp = mesh.shape["tm"], mesh.shape["space"]
    n_x = 4

    def per_device(footprint, block_tile, block_sub, block_rows, obs_var, prior_std, ar_rate, iterate, residual, direction):
        vmem = pl.BlockSpec(memory_space=pltpu.VMEM)
        hbm = pl.BlockSpec(memory_space=pl.ANY)
        slots = pltpu.VMEM((n_sp, CAP, TB, BC), BF16)
        state = pltpu.VMEM((n_tm, SUB, BC), F32)
        vector = jax.ShapeDtypeStruct(iterate.shape, F32)
        begin_iter, begin_res, begin_dir, image, step, ratio = pl.pallas_call(
            functools.partial(kernel, n_tm, n_sp, n_x),
            out_shape=(vector,) * 6,
            in_specs=[hbm] * 10,
            out_specs=(vmem,) * 6,
            scratch_shapes=[
                pltpu.SMEM(block_sub.shape, jnp.int32),
                pltpu.SMEM(block_sub.shape, jnp.int32),
                pltpu.SMEM(block_rows.shape, jnp.int32),
                *[pltpu.VMEM(iterate.shape, F32)] * 4,
                pltpu.VMEM((ROWS, COLS), BF16),
                pltpu.VMEM((ROWS, COLS), F32),
                pltpu.VMEM((ROWS, BC), F32),
                pltpu.VMEM(prior_std.shape, F32),
                pltpu.VMEM(ar_rate.shape, F32),
                pltpu.VMEM((2 * NB * TB, BC), F32),
                pltpu.VMEM((2 * NB, TB, BC), BF16),
                slots, slots, slots, slots, slots, slots, slots, slots,
                pltpu.VMEM((n_sp, 1, BC), jnp.int32),
                pltpu.VMEM((n_sp, 1, BC), jnp.int32),
                pltpu.SMEM((n_sp, 1, BC), jnp.int32),
                pltpu.SMEM((n_sp,), jnp.int32),
                pltpu.SMEM((n_sp,), jnp.int32),
                pltpu.VMEM((SUB * HALF, n_sp * CAP * HALF), BF16),
                pltpu.VMEM((2, SUB * HALF, BC), F32),
                pltpu.VMEM((10, SUB, TB, BC), F32),
                pltpu.VMEM((2, 2, SUB, BC), F32),
                state, state,
                pltpu.VMEM((SUB, BC), F32),
                state,
                pltpu.VMEM((SUB, TB, BC), F32),
                pltpu.VMEM((2, SUB, BC), F32),
                pltpu.VMEM((SUB, TB, BC), BF16),
                pltpu.VMEM((SUB, TB, BC), BF16),
                pltpu.VMEM((NB * TB, BC), F32),
                pltpu.VMEM((1, BC), F32),
                pltpu.VMEM((n_tm, 1, BC), F32),
                pltpu.VMEM((1, BC), F32),
                pltpu.VMEM((n_sp, 1, BC), F32),
                pltpu.SemaphoreType.DMA((CHUNKS + 9,)),
                pltpu.SemaphoreType.DMA((10,)),
                pltpu.SemaphoreType.DMA((10,)),
                pltpu.SemaphoreType.DMA((1,)),
            ],
            compiler_params=pltpu.CompilerParams(
                collective_id=0, has_side_effects=True, vmem_limit_bytes=60 << 20
            ),
            name="cg_step",
        )(
            block_tile.reshape(NB), block_sub, block_rows, footprint.reshape(ROWS, COLS), prior_std, ar_rate,
            obs_var, iterate, residual, direction,
        )
        new_res = begin_res - step * image
        return begin_iter + step * begin_dir, new_res, new_res + ratio * begin_dir

    return jax.shard_map(
        per_device,
        mesh=mesh,
        in_specs=(
            P(("tm", "space"), None, None),
            P(("tm", "space"), None),
            P(("tm", "space")),
            P(("tm", "space")),
            P(None, ("tm", "space")),
            P(None, "tm", "space"),
            P("tm", "space"),
            P(None, ("tm", "space")),
            P(None, ("tm", "space")),
            P(None, ("tm", "space")),
        ),
        out_specs=(P(None, ("tm", "space")), P(None, ("tm", "space")), P(None, ("tm", "space"))),
        check_vma=False,
    )
```

```python
import functools

import jax
import jax.numpy as jnp
from jax import lax
from jax.experimental import pallas as pl
from jax.experimental.pallas import tpu as pltpu
from jax.sharding import PartitionSpec as P

MESH = pl.DeviceIdType.MESH
F32 = jnp.float32
BF16 = jnp.bfloat16

NB, OB, TB, BC, SUB, CAP = 16, 32, 32, 128, 16, 2
ROWS, COLS = NB * OB, TB * BC
HALF = 16
CHUNKS = 4


def kernel(
    n_tm, n_sp, n_x,
    btile_hbm, bsub_hbm, brows_hbm, fp_hbm, prior_hbm, ar_hbm, obs_hbm, iter_hbm, res_hbm, dir_hbm,
    out_iter, out_res, out_dir, out_image, out_step, out_ratio,
    btile, bsub, brows, obs, iterate, residual, direction,
    fp, wide_fp, accum, prior, rate, cbuf, prod, dep1a, dep1b, rcv1a, rcv1b, dep2a, dep2b, rcv2a, rcv2b,
    meta_out, meta_in, meta_smem, first_of, second_of, onehot, back,
    coef, ends, ends_in_a, ends_in_b, rates_own, rates_in, local, carry, fluxa, fluxb, fbuf,
    red_own, red_tm, red_sum, red_sp,
    load_sem, send_sem, recv_sem, smem_sem,
):
    me = lax.axis_index("space")
    mt = lax.axis_index("tm")
    zpos, xpos = me // n_x, me % n_x
    n_z = n_sp // n_x

    def peer(k):
        i = k // n_x
        away = n_z // 2 + (i + 1) // 2 * (1 - 2 * (i % 2))
        return lax.rem(zpos + away, n_z) * n_x + lax.rem(xpos + n_x - 1 - k % n_x, n_x)

    def tpeer(k):
        return lax.rem(mt + k, n_tm)

    width = COLS // CHUNKS
    loads = []
    for c in range(CHUNKS):
        part = pl.ds(c * width, width)
        loads.append(pltpu.make_async_copy(fp_hbm.at[:, part], fp.at[:, part], load_sem.at[c]))
    load_rate = pltpu.make_async_copy(ar_hbm, rate, load_sem.at[CHUNKS])
    load_prior = pltpu.make_async_copy(prior_hbm, prior, load_sem.at[CHUNKS + 1])
    small = [
        pltpu.make_async_copy(src, dst, load_sem.at[CHUNKS + 2 + i])
        for i, (src, dst) in enumerate(
            (
                (btile_hbm, btile), (bsub_hbm, bsub), (brows_hbm, brows), (dir_hbm, direction),
                (res_hbm, residual), (iter_hbm, iterate), (obs_hbm, obs),
            )
        )
    ]
    for copy in small[:4]:
        copy.start()
    for copy in loads:
        copy.start()

    barrier = pltpu.get_barrier_semaphore()

    def greet_space(k, _):
        pl.semaphore_signal(barrier, inc=1, device_id={"space": peer(k)}, device_id_type=MESH)
        return 0

    def greet_tm(k, _):
        pl.semaphore_signal(barrier, inc=1, device_id={"tm": tpeer(k)}, device_id_type=MESH)
        return 0

    lax.fori_loop(0, n_sp - 1, greet_space, 0)
    lax.fori_loop(1, n_tm, greet_tm, 0)
    for copy in small[4:]:
        copy.start()
    load_rate.start()
    load_prior.start()

    for copy in small[:4]:
        copy.wait()

    lane = lax.broadcasted_iota(jnp.int32, (1, ROWS), 1)
    block_of = lane // OB
    limit = jnp.zeros((1, ROWS), jnp.int32)
    for b in range(NB):
        limit = jnp.where(block_of == b, brows[b], limit)
    valid = jnp.where(lane % OB < limit, 1.0, 0.0).astype(F32)
    begin_dir = direction[...] * valid

    tiles = [btile[b] for b in range(NB)]
    place = []
    for b in range(NB):
        count = jnp.int32(0)
        for e in range(b):
            count = count + jnp.where(tiles[e] == tiles[b], 1, 0)
        place.append(jnp.minimum(count, CAP - 1))

    row_j = lax.broadcasted_iota(jnp.int32, (n_sp, BC), 0)
    lane_j = lax.broadcasted_iota(jnp.int32, (n_sp, BC), 1)
    place_j = (lane_j // HALF) % CAP
    wanted = jnp.full((n_sp, BC), -1, jnp.int32)
    for b in range(NB):
        wanted = jnp.where((row_j == tiles[b]) & (place_j == place[b]), bsub[b], wanted)
    meta_out[...] = (wanted * HALF + lane_j % HALF).reshape(n_sp, 1, BC)

    def find(j, _):
        first, second = jnp.int32(0), jnp.int32(0)
        for b in range(NB - 1, -1, -1):
            hit = btile[b] == j
            second = jnp.where(hit, first, second)
            first = jnp.where(hit, b, first)
        first_of[j] = first
        second_of[j] = second
        return 0

    lax.fori_loop(0, n_sp, find, 0)

    rowb = lax.broadcasted_iota(jnp.int32, (NB, ROWS), 0)
    spread = jnp.concatenate(
        [jnp.where(rowb == block_of, begin_dir[r : r + 1, :], 0.0) for r in range(2)], axis=0
    ).astype(BF16)
    for c in range(CHUNKS):
        loads[c].wait()

        got = jnp.dot(spread, fp[:, c * width : (c + 1) * width], preferred_element_type=F32)
        for i in range(width // BC):
            t = c * (width // BC) + i
            cbuf[pl.ds(t, 2 * NB, stride=TB), :] = got[:, i * BC : (i + 1) * BC]

    for i in range(2 * NB):
        prod[i] = cbuf[i * TB : (i + 1) * TB, :].astype(BF16)

    pl.semaphore_wait(barrier, n_sp + n_tm - 2)

    def space_copy(src, dst, j, who, s):
        return pltpu.make_async_remote_copy(
            src_ref=src.at[j], dst_ref=dst.at[who], send_sem=send_sem.at[s], recv_sem=recv_sem.at[s],
            device_id={"space": j}, device_id_type=MESH,
        )

    def tm_copy(src, dst, k, s):
        return pltpu.make_async_remote_copy(
            src_ref=src, dst_ref=dst.at[mt], send_sem=send_sem.at[s], recv_sem=recv_sem.at[s],
            device_id={"tm": k}, device_id_type=MESH,
        )

    def all_arrived(buf, count, s):
        part = buf.at[pl.ds(0, count)]
        pltpu.make_async_copy(part, part, recv_sem.at[s]).wait()

    def all_left(buf, count, s):
        part = buf.at[pl.ds(0, count)]
        pltpu.make_async_copy(part, part, send_sem.at[s]).wait()

    def send_meta(k, _):
        space_copy(meta_out, meta_in, peer(k), me, 0).start()
        return 0


    def fill_first(j):
        dep1a[j, 0] = prod[first_of[j]]
        dep1a[j, 1] = prod[second_of[j]]

    def fill_second(j):
        dep1b[j, 0] = prod[first_of[j] + NB]
        dep1b[j, 1] = prod[second_of[j] + NB]

    def send_first(k, _):
        j = peer(k)
        fill_first(j)
        space_copy(dep1a, rcv1a, j, me, 1).start()
        return 0

    def send_second(k, _):
        j = peer(k)
        fill_second(j)
        space_copy(dep1b, rcv1b, j, me, 2).start()
        return 0

    lax.fori_loop(0, 8, send_first, 0)
    lax.fori_loop(0, n_sp - 1, send_meta, 0)
    meta_in[me] = meta_out[me]
    lax.fori_loop(8, n_sp - 1, send_first, 0)
    fill_first(me)
    rcv1a[me] = dep1a[me]
    lax.fori_loop(0, n_sp - 1, send_second, 0)
    fill_second(me)
    rcv1b[me] = dep1b[me]

    load_rate.wait()
    row8 = lax.broadcasted_iota(jnp.int32, (8, BC), 0)

    def last(v):
        return jnp.broadcast_to(v[7:8, :], (8, BC))

    def head(v):
        return jnp.broadcast_to(v[0:1, :], (8, BC))

    def coefficients(s, _):
        cols = pl.ds(pl.multiple_of(s * BC, BC), BC)
        fcum, bcum = [], []
        for v in range(4):
            a = rate[v * 8 : (v + 1) * 8, cols]
            rows = pl.ds(v * 8, 8)
            c1 = jnp.where(row8 >= 1, a, 0.0)
            p2 = a * jnp.where(row8 >= 1, pltpu.roll(a, 1, 0), 1.0)
            c2 = jnp.where(row8 >= 2, p2, 0.0)
            p4 = p2 * jnp.where(row8 >= 2, pltpu.roll(p2, 2, 0), 1.0)
            c4 = jnp.where(row8 >= 4, p4, 0.0)
            p8 = p4 * jnp.where(row8 >= 4, pltpu.roll(p4, 4, 0), 1.0)
            d1 = jnp.where(row8 <= 6, a, 0.0)
            q2 = a * jnp.where(row8 <= 6, pltpu.roll(a, 7, 0), 1.0)
            d2 = jnp.where(row8 <= 5, q2, 0.0)
            q4 = q2 * jnp.where(row8 <= 5, pltpu.roll(q2, 6, 0), 1.0)
            d4 = jnp.where(row8 <= 3, q4, 0.0)
            q8 = q4 * jnp.where(row8 <= 3, pltpu.roll(q4, 4, 0), 1.0)
            for i, value in enumerate((c1, c2, c4, p8, d1, d2, d4, q8)):
                coef[i, s, rows, :] = value
            fcum.append(p8)
            bcum.append(q8)
        for v in range(1, 4):
            fcum[v] = fcum[v] * last(fcum[v - 1])
        for v in range(2, -1, -1):
            bcum[v] = bcum[v] * head(bcum[v + 1])
        for v in range(4):
            coef[8, s, pl.ds(v * 8, 8), :] = fcum[v]
            above = head(bcum[v + 1]) if v < 3 else jnp.ones((8, BC), F32)
            coef[9, s, pl.ds(v * 8, 8), :] = jnp.where(row8 == 7, above, pltpu.roll(bcum[v], 7, 0))
        rates_own[pl.ds(s, 1), :] = fcum[3][7:8, :]
        return 0

    lax.fori_loop(0, SUB, coefficients, 0)

    def send_rates(k, _):
        tm_copy(rates_own, rates_in, tpeer(k), 3).start()
        return 0

    lax.fori_loop(1, n_tm, send_rates, 0)
    rates_in[mt] = rates_own[...]
    load_prior.wait()

    def widen(t, _):
        at = pl.ds(pl.multiple_of(t * BC, BC), BC)
        wide_fp[:, at] = fp[:, at].astype(F32)
        return 0

    lax.fori_loop(0, TB, widen, 0)

    all_arrived(meta_in, n_sp - 1, 0)
    to_smem = pltpu.make_async_copy(meta_in, meta_smem, smem_sem.at[0])
    to_smem.start()
    quarter = lax.broadcasted_iota(jnp.int32, (1, BC), 1) // (CAP * HALF)
    target = lax.broadcasted_iota(jnp.int32, (SUB * HALF, BC), 0)
    for q in range(n_sp // 4):
        key = meta_in[4 * q]
        for g in range(1, 4):
            key = jnp.where(quarter == g, meta_in[4 * q + g], key)
        onehot[:, q * BC : (q + 1) * BC] = jnp.where(target == key, 1.0, 0.0).astype(BF16)
    to_smem.wait()
    all_arrived(rates_in, n_tm - 1, 3)

    def owner(r, rcv, flux, dep2, ends_in, s_in, s_ends, s_out):
        all_arrived(rcv, n_sp - 1, s_in)
        for h in range(2):
            part = rcv[:, :, h * HALF : (h + 1) * HALF, :].reshape(n_sp * CAP * HALF, BC)
            back[h] = jnp.dot(onehot[...], part, preferred_element_type=F32)

        def recursions(s, _):
            cols = pl.ds(pl.multiple_of(s * BC, BC), BC)
            fwd, bwd = [], []
            for v in range(4):
                rows = pl.ds(v * 8, 8)
                start = pl.multiple_of(s * HALF + (v % 2) * 8, 8)
                term = prior[r, v * 8 : (v + 1) * 8, cols] * back[v // 2, pl.ds(start, 8), :]
                y = term + coef[0, s, rows, :] * pltpu.roll(term, 1, 0)
                y = y + coef[1, s, rows, :] * pltpu.roll(y, 2, 0)
                y = y + coef[2, s, rows, :] * pltpu.roll(y, 4, 0)
                w = term * rate[v * 8 : (v + 1) * 8, cols]
                w = w + coef[4, s, rows, :] * pltpu.roll(w, 7, 0)
                w = w + coef[5, s, rows, :] * pltpu.roll(w, 6, 0)
                w = w + coef[6, s, rows, :] * pltpu.roll(w, 4, 0)
                fwd.append(y)
                bwd.append(w)
            for v in range(1, 4):
                fwd[v] = fwd[v] + coef[3, s, pl.ds(v * 8, 8), :] * last(fwd[v - 1])
            for v in range(2, -1, -1):
                bwd[v] = bwd[v] + coef[7, s, pl.ds(v * 8, 8), :] * head(bwd[v + 1])
            for v in range(4):
                above = head(bwd[v + 1]) if v < 3 else jnp.zeros((8, BC), F32)
                ahead = jnp.where(row8 == 7, above, pltpu.roll(bwd[v], 7, 0))
                local[s, pl.ds(v * 8, 8), :] = fwd[v] + ahead
            ends[r, 0, pl.ds(s, 1), :] = fwd[3][7:8, :]
            ends[r, 1, pl.ds(s, 1), :] = bwd[0][0:1, :]
            return 0

        lax.fori_loop(0, SUB, recursions, 0, unroll=2)

        def send_ends(k, _):
            who = tpeer(k)
            tm_copy(ends.at[r, jnp.where(who > mt, 0, 1)], ends_in, who, s_ends).start()
            return 0

        lax.fori_loop(1, n_tm, send_ends, 0)
        ends_in[mt] = jnp.zeros((SUB, BC), F32)
        all_arrived(ends_in, n_tm - 1, s_ends)
        below = jnp.zeros((SUB, BC), F32)
        for i in range(n_tm - 1):
            below = jnp.where(i < mt, rates_in[i] * below + ends_in[i], below)
        above = jnp.zeros((SUB, BC), F32)
        for i in range(n_tm - 1, 0, -1):
            above = jnp.where(i > mt, rates_in[i] * above + ends_in[i], above)
        carry[0] = below
        carry[1] = above

        def finish(s, _):
            cols = pl.ds(pl.multiple_of(s * BC, BC), BC)
            total = (
                local[s]
                + coef[8, s] * carry[0, pl.ds(s, 1), :]
                + coef[9, s] * carry[1, pl.ds(s, 1), :]
            )
            flux[s] = (prior[r, :, cols] * total).astype(BF16)
            return 0

        lax.fori_loop(0, SUB, finish, 0, unroll=2)

        def fill(j):
            for p in range(CAP):
                dep2[j, p] = flux[jnp.maximum(meta_smem[j, 0, p * HALF], 0) // HALF]

        def send_flux(k, _):
            j = peer(k)
            fill(j)
            space_copy(dep2, rcv2a if r == 0 else rcv2b, j, me, s_out).start()
            return 0

        lax.fori_loop(0, n_sp - 1, send_flux, 0)
        fill(me)
        (rcv2a if r == 0 else rcv2b)[me] = dep2[me]

    owner(0, rcv1a, fluxa, dep2a, ends_in_a, 1, 4, 6)
    owner(1, rcv1b, fluxb, dep2b, ends_in_b, 2, 5, 7)

    for copy in small[4:]:
        copy.wait()
    begin_res = residual[...] * valid

    images = []
    for r, (rcv, s_out) in enumerate(((rcv2a, 6), (rcv2b, 7))):
        all_arrived(rcv, n_sp - 1, s_out)
        for b in range(NB):
            fbuf[b * TB : (b + 1) * TB, :] = rcv[tiles[b], place[b]].astype(F32)

        def project(b, _):
            own = pl.ds(pl.multiple_of(b * OB, OB), OB)
            total = jnp.zeros((OB, BC), F32)
            for t in range(TB):
                total = total + wide_fp[own, t * BC : (t + 1) * BC] * fbuf[pl.ds(b * TB + t, 1), :]
            accum[own, :] = total
            return 0

        lax.fori_loop(0, NB, project, 0, unroll=2)
        images.append(
            jnp.concatenate(
                [
                    jnp.sum(accum[i * BC : (i + 1) * BC, :].T, axis=0, keepdims=True)
                    for i in range(ROWS // BC)
                ],
                axis=1,
            )
        )
    image = jnp.concatenate(images, axis=0) * valid + obs[...] * begin_dir

    def partial(value):
        total = value[:, :BC]
        for i in range(1, ROWS // BC):
            total = total + value[:, i * BC : (i + 1) * BC]
        return total

    mine = jnp.concatenate(
        [
            partial(begin_res * begin_res),
            partial(begin_dir * image),
            partial(begin_res * image),
            partial(image * image),
        ],
        axis=0,
    )
    lane8 = lax.broadcasted_iota(jnp.int32, (8, BC), 1)
    row8 = lax.broadcasted_iota(jnp.int32, (8, BC), 0)

    def as_row(column):
        return jnp.sum(jnp.where(lane8 == row8, column, 0.0), axis=0, keepdims=True)

    mine = as_row(jnp.sum(mine, axis=1, keepdims=True))
    red_own[...] = mine
    red_tm[mt] = mine

    def send_tm_sum(k, _):
        tm_copy(red_own, red_tm, tpeer(k), 8).start()
        return 0

    lax.fori_loop(1, n_tm, send_tm_sum, 0)
    all_arrived(red_tm, n_tm - 1, 8)
    part = red_tm[0]
    for i in range(1, n_tm):
        part = part + red_tm[i]
    red_sum[...] = part
    red_sp[me] = part

    def send_sp_sum(k, _):
        pltpu.make_async_remote_copy(
            src_ref=red_sum, dst_ref=red_sp.at[me], send_sem=send_sem.at[9], recv_sem=recv_sem.at[9],
            device_id={"space": peer(k)}, device_id_type=MESH,
        ).start()
        return 0

    lax.fori_loop(0, n_sp - 1, send_sp_sum, 0)
    all_arrived(red_sp, n_sp - 1, 9)
    whole = jnp.broadcast_to(jnp.sum(red_sp[...], axis=0), (8, BC))
    whole = jnp.sum(jnp.where(lane8 == row8, whole, 0.0), axis=1, keepdims=True)
    res_norm, curvature, cross, square = (whole[2 * i : 2 * i + 2, :] for i in range(4))
    step = res_norm / curvature
    next_norm = res_norm - 2.0 * step * cross + step * step * square
    wide = begin_dir.shape
    out_iter[...] = iterate[...] * valid
    out_res[...] = begin_res
    out_dir[...] = begin_dir
    out_image[...] = image
    out_step[...] = jnp.broadcast_to(step, wide)
    out_ratio[...] = jnp.broadcast_to(next_norm / res_norm, wide)

    all_left(meta_out, n_sp - 1, 0)
    all_left(dep1a, n_sp - 1, 1)
    all_left(dep1b, n_sp - 1, 2)
    all_left(rates_in, n_tm - 1, 3)
    all_left(ends_in_a, n_tm - 1, 4)
    all_left(ends_in_b, n_tm - 1, 5)
    all_left(dep2a, n_sp - 1, 6)
    all_left(dep2b, n_sp - 1, 7)
    all_left(red_tm, n_tm - 1, 8)
    all_left(red_sp, n_sp - 1, 9)


def solution(mesh):
    n_tm, n_sp = mesh.shape["tm"], mesh.shape["space"]
    n_x = 4

    def per_device(footprint, block_tile, block_sub, block_rows, obs_var, prior_std, ar_rate, iterate, residual, direction):
        vmem = pl.BlockSpec(memory_space=pltpu.VMEM)
        hbm = pl.BlockSpec(memory_space=pl.ANY)
        slots = pltpu.VMEM((n_sp, CAP, TB, BC), BF16)
        state = pltpu.VMEM((n_tm, SUB, BC), F32)
        vector = jax.ShapeDtypeStruct(iterate.shape, F32)
        begin_iter, begin_res, begin_dir, image, step, ratio = pl.pallas_call(
            functools.partial(kernel, n_tm, n_sp, n_x),
            out_shape=(vector,) * 6,
            in_specs=[hbm] * 10,
            out_specs=(vmem,) * 6,
            scratch_shapes=[
                pltpu.SMEM(block_sub.shape, jnp.int32),
                pltpu.SMEM(block_sub.shape, jnp.int32),
                pltpu.SMEM(block_rows.shape, jnp.int32),
                *[pltpu.VMEM(iterate.shape, F32)] * 4,
                pltpu.VMEM((ROWS, COLS), BF16),
                pltpu.VMEM((ROWS, COLS), F32),
                pltpu.VMEM((ROWS, BC), F32),
                pltpu.VMEM(prior_std.shape, F32),
                pltpu.VMEM(ar_rate.shape, F32),
                pltpu.VMEM((2 * NB * TB, BC), F32),
                pltpu.VMEM((2 * NB, TB, BC), BF16),
                slots, slots, slots, slots, slots, slots, slots, slots,
                pltpu.VMEM((n_sp, 1, BC), jnp.int32),
                pltpu.VMEM((n_sp, 1, BC), jnp.int32),
                pltpu.SMEM((n_sp, 1, BC), jnp.int32),
                pltpu.SMEM((n_sp,), jnp.int32),
                pltpu.SMEM((n_sp,), jnp.int32),
                pltpu.VMEM((SUB * HALF, n_sp * CAP * HALF), BF16),
                pltpu.VMEM((2, SUB * HALF, BC), F32),
                pltpu.VMEM((10, SUB, TB, BC), F32),
                pltpu.VMEM((2, 2, SUB, BC), F32),
                state, state,
                pltpu.VMEM((SUB, BC), F32),
                state,
                pltpu.VMEM((SUB, TB, BC), F32),
                pltpu.VMEM((2, SUB, BC), F32),
                pltpu.VMEM((SUB, TB, BC), BF16),
                pltpu.VMEM((SUB, TB, BC), BF16),
                pltpu.VMEM((NB * TB, BC), F32),
                pltpu.VMEM((1, BC), F32),
                pltpu.VMEM((n_tm, 1, BC), F32),
                pltpu.VMEM((1, BC), F32),
                pltpu.VMEM((n_sp, 1, BC), F32),
                pltpu.SemaphoreType.DMA((CHUNKS + 9,)),
                pltpu.SemaphoreType.DMA((10,)),
                pltpu.SemaphoreType.DMA((10,)),
                pltpu.SemaphoreType.DMA((1,)),
            ],
            compiler_params=pltpu.CompilerParams(
                collective_id=0, has_side_effects=True, vmem_limit_bytes=60 << 20
            ),
            name="cg_step",
        )(
            block_tile.reshape(NB), block_sub, block_rows, footprint.reshape(ROWS, COLS), prior_std, ar_rate,
            obs_var, iterate, residual, direction,
        )
        new_res = begin_res - step * image
        return begin_iter + step * begin_dir, new_res, new_res + ratio * begin_dir

    return jax.shard_map(
        per_device,
        mesh=mesh,
        in_specs=(
            P(("tm", "space"), None, None),
            P(("tm", "space"), None),
            P(("tm", "space")),
            P(("tm", "space")),
            P(None, ("tm", "space")),
            P(None, "tm", "space"),
            P("tm", "space"),
            P(None, ("tm", "space")),
            P(None, ("tm", "space")),
            P(None, ("tm", "space")),
        ),
        out_specs=(P(None, ("tm", "space")), P(None, ("tm", "space")), P(None, ("tm", "space"))),
        check_vma=False,
    )
```

```python
import functools

import jax
import jax.numpy as jnp
from jax import lax
from jax.experimental import pallas as pl
from jax.experimental.pallas import tpu as pltpu
from jax.sharding import PartitionSpec as P

MESH = pl.DeviceIdType.MESH
F32 = jnp.float32
BF16 = jnp.bfloat16

NB, OB, TB, BC, SUB, CAP = 16, 32, 32, 128, 16, 2
ROWS, COLS = NB * OB, TB * BC
HALF = 16
CHUNKS = 4


def kernel(
    n_tm, n_sp, n_x,
    btile_hbm, bsub_hbm, brows_hbm, fp_hbm, prior_hbm, ar_hbm, obs_hbm, iter_hbm, res_hbm, dir_hbm,
    out_iter, out_res, out_dir, out_image, out_step, out_ratio,
    btile, bsub, brows, obs, iterate, residual, direction,
    fp, wide_fp, accum, prior, rate, cbuf, prod, dep1a, dep1b, rcv1a, rcv1b, dep2a, dep2b, rcv2a, rcv2b,
    meta_out, meta_in, meta_smem, first_of, second_of, onehot, back,
    coef, ends, ends_in_a, ends_in_b, rates_own, rates_in, local, carry, fluxa, fluxb, fbuf,
    red_own, red_tm, red_sum, red_sp,
    load_sem, send_sem, recv_sem, smem_sem,
):
    me = lax.axis_index("space")
    mt = lax.axis_index("tm")
    zpos, xpos = me // n_x, me % n_x
    n_z = n_sp // n_x

    def peer(k):
        i = k % n_z
        away = n_z // 2 + (i + 1) // 2 * (1 - 2 * (i % 2))
        return lax.rem(zpos + away, n_z) * n_x + lax.rem(xpos + n_x - 1 - k // n_z, n_x)

    def tpeer(k):
        return lax.rem(mt + k, n_tm)

    width = COLS // CHUNKS
    loads = []
    for c in range(CHUNKS):
        part = pl.ds(c * width, width)
        loads.append(pltpu.make_async_copy(fp_hbm.at[:, part], fp.at[:, part], load_sem.at[c]))
    load_rate = pltpu.make_async_copy(ar_hbm, rate, load_sem.at[CHUNKS])
    load_prior = pltpu.make_async_copy(prior_hbm, prior, load_sem.at[CHUNKS + 1])
    small = [
        pltpu.make_async_copy(src, dst, load_sem.at[CHUNKS + 2 + i])
        for i, (src, dst) in enumerate(
            (
                (btile_hbm, btile), (bsub_hbm, bsub), (brows_hbm, brows), (dir_hbm, direction),
                (res_hbm, residual), (iter_hbm, iterate), (obs_hbm, obs),
            )
        )
    ]
    for copy in small[:4]:
        copy.start()
    for copy in loads:
        copy.start()

    barrier = pltpu.get_barrier_semaphore()

    def greet_space(k, _):
        pl.semaphore_signal(barrier, inc=1, device_id={"space": peer(k)}, device_id_type=MESH)
        return 0

    def greet_tm(k, _):
        pl.semaphore_signal(barrier, inc=1, device_id={"tm": tpeer(k)}, device_id_type=MESH)
        return 0

    lax.fori_loop(0, n_sp - 1, greet_space, 0)
    lax.fori_loop(1, n_tm, greet_tm, 0)
    for copy in small[4:]:
        copy.start()
    load_rate.start()
    load_prior.start()

    for copy in small[:4]:
        copy.wait()

    lane = lax.broadcasted_iota(jnp.int32, (1, ROWS), 1)
    block_of = lane // OB
    limit = jnp.zeros((1, ROWS), jnp.int32)
    for b in range(NB):
        limit = jnp.where(block_of == b, brows[b], limit)
    valid = jnp.where(lane % OB < limit, 1.0, 0.0).astype(F32)
    begin_dir = direction[...] * valid

    tiles = [btile[b] for b in range(NB)]
    place = []
    for b in range(NB):
        count = jnp.int32(0)
        for e in range(b):
            count = count + jnp.where(tiles[e] == tiles[b], 1, 0)
        place.append(jnp.minimum(count, CAP - 1))

    row_j = lax.broadcasted_iota(jnp.int32, (n_sp, BC), 0)
    lane_j = lax.broadcasted_iota(jnp.int32, (n_sp, BC), 1)
    place_j = (lane_j // HALF) % CAP
    wanted = jnp.full((n_sp, BC), -1, jnp.int32)
    for b in range(NB):
        wanted = jnp.where((row_j == tiles[b]) & (place_j == place[b]), bsub[b], wanted)
    meta_out[...] = (wanted * HALF + lane_j % HALF).reshape(n_sp, 1, BC)

    def find(j, _):
        first, second = jnp.int32(0), jnp.int32(0)
        for b in range(NB - 1, -1, -1):
            hit = btile[b] == j
            second = jnp.where(hit, first, second)
            first = jnp.where(hit, b, first)
        first_of[j] = first
        second_of[j] = second
        return 0

    lax.fori_loop(0, n_sp, find, 0)

    rowb = lax.broadcasted_iota(jnp.int32, (NB, ROWS), 0)
    spread = jnp.concatenate(
        [jnp.where(rowb == block_of, begin_dir[r : r + 1, :], 0.0) for r in range(2)], axis=0
    ).astype(BF16)
    for c in range(CHUNKS):
        loads[c].wait()

        got = jnp.dot(spread, fp[:, c * width : (c + 1) * width], preferred_element_type=F32)
        for i in range(width // BC):
            t = c * (width // BC) + i
            cbuf[pl.ds(t, 2 * NB, stride=TB), :] = got[:, i * BC : (i + 1) * BC]

    for i in range(2 * NB):
        prod[i] = cbuf[i * TB : (i + 1) * TB, :].astype(BF16)

    pl.semaphore_wait(barrier, n_sp + n_tm - 2)

    def space_copy(src, dst, j, who, s):
        return pltpu.make_async_remote_copy(
            src_ref=src.at[j], dst_ref=dst.at[who], send_sem=send_sem.at[s], recv_sem=recv_sem.at[s],
            device_id={"space": j}, device_id_type=MESH,
        )

    def tm_copy(src, dst, k, s):
        return pltpu.make_async_remote_copy(
            src_ref=src, dst_ref=dst.at[mt], send_sem=send_sem.at[s], recv_sem=recv_sem.at[s],
            device_id={"tm": k}, device_id_type=MESH,
        )

    def all_arrived(buf, count, s):
        part = buf.at[pl.ds(0, count)]
        pltpu.make_async_copy(part, part, recv_sem.at[s]).wait()

    def all_left(buf, count, s):
        part = buf.at[pl.ds(0, count)]
        pltpu.make_async_copy(part, part, send_sem.at[s]).wait()

    def send_meta(k, _):
        space_copy(meta_out, meta_in, peer(k), me, 0).start()
        return 0


    def fill_first(j):
        dep1a[j, 0] = prod[first_of[j]]
        dep1a[j, 1] = prod[second_of[j]]

    def fill_second(j):
        dep1b[j, 0] = prod[first_of[j] + NB]
        dep1b[j, 1] = prod[second_of[j] + NB]

    def send_first(k, _):
        j = peer(k)
        fill_first(j)
        space_copy(dep1a, rcv1a, j, me, 1).start()
        return 0

    def send_second(k, _):
        j = peer(k)
        fill_second(j)
        space_copy(dep1b, rcv1b, j, me, 2).start()
        return 0

    lax.fori_loop(0, 8, send_first, 0)
    lax.fori_loop(0, n_sp - 1, send_meta, 0)
    meta_in[me] = meta_out[me]
    lax.fori_loop(8, n_sp - 1, send_first, 0)
    fill_first(me)
    rcv1a[me] = dep1a[me]
    lax.fori_loop(0, n_sp - 1, send_second, 0)
    fill_second(me)
    rcv1b[me] = dep1b[me]

    load_rate.wait()
    row8 = lax.broadcasted_iota(jnp.int32, (8, BC), 0)

    def last(v):
        return jnp.broadcast_to(v[7:8, :], (8, BC))

    def head(v):
        return jnp.broadcast_to(v[0:1, :], (8, BC))

    def coefficients(s, _):
        cols = pl.ds(pl.multiple_of(s * BC, BC), BC)
        fcum, bcum = [], []
        for v in range(4):
            a = rate[v * 8 : (v + 1) * 8, cols]
            rows = pl.ds(v * 8, 8)
            c1 = jnp.where(row8 >= 1, a, 0.0)
            p2 = a * jnp.where(row8 >= 1, pltpu.roll(a, 1, 0), 1.0)
            c2 = jnp.where(row8 >= 2, p2, 0.0)
            p4 = p2 * jnp.where(row8 >= 2, pltpu.roll(p2, 2, 0), 1.0)
            c4 = jnp.where(row8 >= 4, p4, 0.0)
            p8 = p4 * jnp.where(row8 >= 4, pltpu.roll(p4, 4, 0), 1.0)
            d1 = jnp.where(row8 <= 6, a, 0.0)
            q2 = a * jnp.where(row8 <= 6, pltpu.roll(a, 7, 0), 1.0)
            d2 = jnp.where(row8 <= 5, q2, 0.0)
            q4 = q2 * jnp.where(row8 <= 5, pltpu.roll(q2, 6, 0), 1.0)
            d4 = jnp.where(row8 <= 3, q4, 0.0)
            q8 = q4 * jnp.where(row8 <= 3, pltpu.roll(q4, 4, 0), 1.0)
            for i, value in enumerate((c1, c2, c4, p8, d1, d2, d4, q8)):
                coef[i, s, rows, :] = value
            fcum.append(p8)
            bcum.append(q8)
        for v in range(1, 4):
            fcum[v] = fcum[v] * last(fcum[v - 1])
        for v in range(2, -1, -1):
            bcum[v] = bcum[v] * head(bcum[v + 1])
        for v in range(4):
            coef[8, s, pl.ds(v * 8, 8), :] = fcum[v]
            above = head(bcum[v + 1]) if v < 3 else jnp.ones((8, BC), F32)
            coef[9, s, pl.ds(v * 8, 8), :] = jnp.where(row8 == 7, above, pltpu.roll(bcum[v], 7, 0))
        rates_own[pl.ds(s, 1), :] = fcum[3][7:8, :]
        return 0

    lax.fori_loop(0, SUB, coefficients, 0)

    def send_rates(k, _):
        tm_copy(rates_own, rates_in, tpeer(k), 3).start()
        return 0

    lax.fori_loop(1, n_tm, send_rates, 0)
    rates_in[mt] = rates_own[...]
    load_prior.wait()

    def widen(t, _):
        at = pl.ds(pl.multiple_of(t * BC, BC), BC)
        wide_fp[:, at] = fp[:, at].astype(F32)
        return 0

    lax.fori_loop(0, TB, widen, 0)

    all_arrived(meta_in, n_sp - 1, 0)
    to_smem = pltpu.make_async_copy(meta_in, meta_smem, smem_sem.at[0])
    to_smem.start()
    quarter = lax.broadcasted_iota(jnp.int32, (1, BC), 1) // (CAP * HALF)
    target = lax.broadcasted_iota(jnp.int32, (SUB * HALF, BC), 0)
    for q in range(n_sp // 4):
        key = meta_in[4 * q]
        for g in range(1, 4):
            key = jnp.where(quarter == g, meta_in[4 * q + g], key)
        onehot[:, q * BC : (q + 1) * BC] = jnp.where(target == key, 1.0, 0.0).astype(BF16)
    to_smem.wait()
    all_arrived(rates_in, n_tm - 1, 3)

    def owner(r, rcv, flux, dep2, ends_in, s_in, s_ends, s_out):
        all_arrived(rcv, n_sp - 1, s_in)
        for h in range(2):
            part = rcv[:, :, h * HALF : (h + 1) * HALF, :].reshape(n_sp * CAP * HALF, BC)
            back[h] = jnp.dot(onehot[...], part, preferred_element_type=F32)

        def recursions(s, _):
            cols = pl.ds(pl.multiple_of(s * BC, BC), BC)
            fwd, bwd = [], []
            for v in range(4):
                rows = pl.ds(v * 8, 8)
                start = pl.multiple_of(s * HALF + (v % 2) * 8, 8)
                term = prior[r, v * 8 : (v + 1) * 8, cols] * back[v // 2, pl.ds(start, 8), :]
                y = term + coef[0, s, rows, :] * pltpu.roll(term, 1, 0)
                y = y + coef[1, s, rows, :] * pltpu.roll(y, 2, 0)
                y = y + coef[2, s, rows, :] * pltpu.roll(y, 4, 0)
                w = term * rate[v * 8 : (v + 1) * 8, cols]
                w = w + coef[4, s, rows, :] * pltpu.roll(w, 7, 0)
                w = w + coef[5, s, rows, :] * pltpu.roll(w, 6, 0)
                w = w + coef[6, s, rows, :] * pltpu.roll(w, 4, 0)
                fwd.append(y)
                bwd.append(w)
            for v in range(1, 4):
                fwd[v] = fwd[v] + coef[3, s, pl.ds(v * 8, 8), :] * last(fwd[v - 1])
            for v in range(2, -1, -1):
                bwd[v] = bwd[v] + coef[7, s, pl.ds(v * 8, 8), :] * head(bwd[v + 1])
            for v in range(4):
                above = head(bwd[v + 1]) if v < 3 else jnp.zeros((8, BC), F32)
                ahead = jnp.where(row8 == 7, above, pltpu.roll(bwd[v], 7, 0))
                local[s, pl.ds(v * 8, 8), :] = fwd[v] + ahead
            ends[r, 0, pl.ds(s, 1), :] = fwd[3][7:8, :]
            ends[r, 1, pl.ds(s, 1), :] = bwd[0][0:1, :]
            return 0

        lax.fori_loop(0, SUB, recursions, 0, unroll=2)

        def send_ends(k, _):
            who = tpeer(k)
            tm_copy(ends.at[r, jnp.where(who > mt, 0, 1)], ends_in, who, s_ends).start()
            return 0

        lax.fori_loop(1, n_tm, send_ends, 0)
        ends_in[mt] = jnp.zeros((SUB, BC), F32)
        all_arrived(ends_in, n_tm - 1, s_ends)
        below = jnp.zeros((SUB, BC), F32)
        for i in range(n_tm - 1):
            below = jnp.where(i < mt, rates_in[i] * below + ends_in[i], below)
        above = jnp.zeros((SUB, BC), F32)
        for i in range(n_tm - 1, 0, -1):
            above = jnp.where(i > mt, rates_in[i] * above + ends_in[i], above)
        carry[0] = below
        carry[1] = above

        def finish(s, _):
            cols = pl.ds(pl.multiple_of(s * BC, BC), BC)
            total = (
                local[s]
                + coef[8, s] * carry[0, pl.ds(s, 1), :]
                + coef[9, s] * carry[1, pl.ds(s, 1), :]
            )
            flux[s] = (prior[r, :, cols] * total).astype(BF16)
            return 0

        lax.fori_loop(0, SUB, finish, 0, unroll=2)

        def fill(j):
            for p in range(CAP):
                dep2[j, p] = flux[jnp.maximum(meta_smem[j, 0, p * HALF], 0) // HALF]

        def send_flux(k, _):
            j = peer(k)
            fill(j)
            space_copy(dep2, rcv2a if r == 0 else rcv2b, j, me, s_out).start()
            return 0

        lax.fori_loop(0, n_sp - 1, send_flux, 0)
        fill(me)
        (rcv2a if r == 0 else rcv2b)[me] = dep2[me]

    owner(0, rcv1a, fluxa, dep2a, ends_in_a, 1, 4, 6)
    owner(1, rcv1b, fluxb, dep2b, ends_in_b, 2, 5, 7)

    for copy in small[4:]:
        copy.wait()
    begin_res = residual[...] * valid

    images = []
    for r, (rcv, s_out) in enumerate(((rcv2a, 6), (rcv2b, 7))):
        all_arrived(rcv, n_sp - 1, s_out)
        for b in range(NB):
            fbuf[b * TB : (b + 1) * TB, :] = rcv[tiles[b], place[b]].astype(F32)

        def project(b, _):
            own = pl.ds(pl.multiple_of(b * OB, OB), OB)
            total = jnp.zeros((OB, BC), F32)
            for t in range(TB):
                total = total + wide_fp[own, t * BC : (t + 1) * BC] * fbuf[pl.ds(b * TB + t, 1), :]
            accum[own, :] = total
            return 0

        lax.fori_loop(0, NB, project, 0, unroll=2)
        images.append(
            jnp.concatenate(
                [
                    jnp.sum(accum[i * BC : (i + 1) * BC, :].T, axis=0, keepdims=True)
                    for i in range(ROWS // BC)
                ],
                axis=1,
            )
        )
    image = jnp.concatenate(images, axis=0) * valid + obs[...] * begin_dir

    def partial(value):
        total = value[:, :BC]
        for i in range(1, ROWS // BC):
            total = total + value[:, i * BC : (i + 1) * BC]
        return total

    mine = jnp.concatenate(
        [
            partial(begin_res * begin_res),
            partial(begin_dir * image),
            partial(begin_res * image),
            partial(image * image),
        ],
        axis=0,
    )
    lane8 = lax.broadcasted_iota(jnp.int32, (8, BC), 1)
    row8 = lax.broadcasted_iota(jnp.int32, (8, BC), 0)

    def as_row(column):
        return jnp.sum(jnp.where(lane8 == row8, column, 0.0), axis=0, keepdims=True)

    mine = as_row(jnp.sum(mine, axis=1, keepdims=True))
    red_own[...] = mine
    red_tm[mt] = mine

    def send_tm_sum(k, _):
        tm_copy(red_own, red_tm, tpeer(k), 8).start()
        return 0

    lax.fori_loop(1, n_tm, send_tm_sum, 0)
    all_arrived(red_tm, n_tm - 1, 8)
    part = red_tm[0]
    for i in range(1, n_tm):
        part = part + red_tm[i]
    red_sum[...] = part
    red_sp[me] = part

    def send_sp_sum(k, _):
        pltpu.make_async_remote_copy(
            src_ref=red_sum, dst_ref=red_sp.at[me], send_sem=send_sem.at[9], recv_sem=recv_sem.at[9],
            device_id={"space": peer(k)}, device_id_type=MESH,
        ).start()
        return 0

    lax.fori_loop(0, n_sp - 1, send_sp_sum, 0)
    all_left(meta_out, n_sp - 1, 0)
    all_left(dep1a, n_sp - 1, 1)
    all_left(dep1b, n_sp - 1, 2)
    all_left(rates_in, n_tm - 1, 3)
    all_left(ends_in_a, n_tm - 1, 4)
    all_left(ends_in_b, n_tm - 1, 5)
    all_left(dep2a, n_sp - 1, 6)
    all_left(dep2b, n_sp - 1, 7)
    all_left(red_tm, n_tm - 1, 8)
    all_left(red_sp, n_sp - 1, 9)
    all_arrived(red_sp, n_sp - 1, 9)
    whole = jnp.broadcast_to(jnp.sum(red_sp[...], axis=0), (8, BC))
    whole = jnp.sum(jnp.where(lane8 == row8, whole, 0.0), axis=1, keepdims=True)
    res_norm, curvature, cross, square = (whole[2 * i : 2 * i + 2, :] for i in range(4))
    step = res_norm / curvature
    next_norm = res_norm - 2.0 * step * cross + step * step * square
    wide = begin_dir.shape
    out_iter[...] = iterate[...] * valid
    out_res[...] = begin_res
    out_dir[...] = begin_dir
    out_image[...] = image
    out_step[...] = jnp.broadcast_to(step, wide)
    out_ratio[...] = jnp.broadcast_to(next_norm / res_norm, wide)


def solution(mesh):
    n_tm, n_sp = mesh.shape["tm"], mesh.shape["space"]
    n_x = 4

    def per_device(footprint, block_tile, block_sub, block_rows, obs_var, prior_std, ar_rate, iterate, residual, direction):
        vmem = pl.BlockSpec(memory_space=pltpu.VMEM)
        hbm = pl.BlockSpec(memory_space=pl.ANY)
        slots = pltpu.VMEM((n_sp, CAP, TB, BC), BF16)
        state = pltpu.VMEM((n_tm, SUB, BC), F32)
        vector = jax.ShapeDtypeStruct(iterate.shape, F32)
        begin_iter, begin_res, begin_dir, image, step, ratio = pl.pallas_call(
            functools.partial(kernel, n_tm, n_sp, n_x),
            out_shape=(vector,) * 6,
            in_specs=[hbm] * 10,
            out_specs=(vmem,) * 6,
            scratch_shapes=[
                pltpu.SMEM(block_sub.shape, jnp.int32),
                pltpu.SMEM(block_sub.shape, jnp.int32),
                pltpu.SMEM(block_rows.shape, jnp.int32),
                *[pltpu.VMEM(iterate.shape, F32)] * 4,
                pltpu.VMEM((ROWS, COLS), BF16),
                pltpu.VMEM((ROWS, COLS), F32),
                pltpu.VMEM((ROWS, BC), F32),
                pltpu.VMEM(prior_std.shape, F32),
                pltpu.VMEM(ar_rate.shape, F32),
                pltpu.VMEM((2 * NB * TB, BC), F32),
                pltpu.VMEM((2 * NB, TB, BC), BF16),
                slots, slots, slots, slots, slots, slots, slots, slots,
                pltpu.VMEM((n_sp, 1, BC), jnp.int32),
                pltpu.VMEM((n_sp, 1, BC), jnp.int32),
                pltpu.SMEM((n_sp, 1, BC), jnp.int32),
                pltpu.SMEM((n_sp,), jnp.int32),
                pltpu.SMEM((n_sp,), jnp.int32),
                pltpu.VMEM((SUB * HALF, n_sp * CAP * HALF), BF16),
                pltpu.VMEM((2, SUB * HALF, BC), F32),
                pltpu.VMEM((10, SUB, TB, BC), F32),
                pltpu.VMEM((2, 2, SUB, BC), F32),
                state, state,
                pltpu.VMEM((SUB, BC), F32),
                state,
                pltpu.VMEM((SUB, TB, BC), F32),
                pltpu.VMEM((2, SUB, BC), F32),
                pltpu.VMEM((SUB, TB, BC), BF16),
                pltpu.VMEM((SUB, TB, BC), BF16),
                pltpu.VMEM((NB * TB, BC), F32),
                pltpu.VMEM((1, BC), F32),
                pltpu.VMEM((n_tm, 1, BC), F32),
                pltpu.VMEM((1, BC), F32),
                pltpu.VMEM((n_sp, 1, BC), F32),
                pltpu.SemaphoreType.DMA((CHUNKS + 9,)),
                pltpu.SemaphoreType.DMA((10,)),
                pltpu.SemaphoreType.DMA((10,)),
                pltpu.SemaphoreType.DMA((1,)),
            ],
            compiler_params=pltpu.CompilerParams(
                collective_id=0, has_side_effects=True, vmem_limit_bytes=60 << 20
            ),
            name="cg_step",
        )(
            block_tile.reshape(NB), block_sub, block_rows, footprint.reshape(ROWS, COLS), prior_std, ar_rate,
            obs_var, iterate, residual, direction,
        )
        new_res = begin_res - step * image
        return begin_iter + step * begin_dir, new_res, new_res + ratio * begin_dir

    return jax.shard_map(
        per_device,
        mesh=mesh,
        in_specs=(
            P(("tm", "space"), None, None),
            P(("tm", "space"), None),
            P(("tm", "space")),
            P(("tm", "space")),
            P(None, ("tm", "space")),
            P(None, "tm", "space"),
            P("tm", "space"),
            P(None, ("tm", "space")),
            P(None, ("tm", "space")),
            P(None, ("tm", "space")),
        ),
        out_specs=(P(None, ("tm", "space")), P(None, ("tm", "space")), P(None, ("tm", "space"))),
        check_vma=False,
    )
```
